32 devices in a mesh: enc: 4 (over y, x), dp: 4 (over z), rep: 2 (over core).
Axes of the slice: x: 2, y: 2, z: 4, core: 2. Of those that a mesh axis runs over, the one named last changes fastest.
Arguments:
- feat_sig: bfloat16 [128, 1152], P(('dp', 'rep'), 'enc'), may hold values from -6 to 6
- feat_cnx: bfloat16 [128, 3072], P(('dp', 'rep'), 'enc'), may hold values from -6 to 6
- cotangent: bfloat16 [128, 2048], P(('dp', 'rep'), 'enc'), may hold values from -6 to 6
- w_sig: bfloat16 [2048, 1152], P(None, 'enc'), may hold values from -0.09375 to 0.09375
- w_cnx: bfloat16 [2048, 3072], P(None, 'enc'), may hold values from -0.09375 to 0.09375
- lengths: int32 [8, 4], P(('dp', 'rep')), may hold values from 1 to 4, as said below
- enc_of: int32 [8, 4], P(('dp', 'rep')), may hold values from 0 to 3, each once within a row
- owner_of: int32 [8, 4], P(('dp', 'rep')), may hold values from 0 to 3, each once within a row
- pre_sig: bfloat16 [128, 1152], P(('dp', 'rep'), 'enc'), may hold values from -6 to 6
- pre_cnx: bfloat16 [128, 3072], P(('dp', 'rep'), 'enc'), may hold values from -6 to 6
- gain_sig: float32 [1152], P('enc'), may hold values from 0.5 to 2
- gain_cnx: float32 [3072], P('enc'), may hold values from 0.5 to 2
Outputs:
- grad_w_sig: float32 [2048, 1152], P(('dp', 'rep'), 'enc')
- grad_w_cnx: float32 [2048, 3072], P(('dp', 'rep'), 'enc')
- gradient_before_siglip: bfloat16 [128, 1152], P(('dp', 'rep'), 'enc')
- gradient_before_convnext: bfloat16 [128, 3072], P(('dp', 'rep'), 'enc')
The draws below stay inside these ranges and needn't reach their ends.
Inputs may be any that keep to these rules, and one draw needn't show every extreme that they name: `lengths`: every entry is 1, 2, 3 or 4; every row holds at least one entry equal to 4. `enc_of`: each row is a permutation of 0 .. 3. `owner_of`: each row is a permutation of 0 .. 3.
All inputs are finite; a program needn't handle non-finite values.
Results may differ from the reference program's by a relative error of at most 0.0049.
Values may be sent and summed in bfloat16 or wider, within the bound.
A program may use at most 64 MiB of HBM per device.

```python
import math
import jax
import jax.numpy as jnp
from jax import lax

D = 2048
C_SIG = 1152
C_CNX = 3072
CAP = 4
TOKENS = 128
N_DP = 4
N_REP = 2


def draw_lengths(key, part):
    key = jax.random.fold_in(key, 7)
    owners = N_DP * N_REP
    units = jax.random.randint(key, (owners, N_DP), 1, 5)
    longest = jax.random.randint(jax.random.fold_in(key, 1), (owners, 1), 0, N_DP)
    columns = lax.broadcasted_iota(jnp.int32, (owners, N_DP), 1)
    units = jnp.where(columns == longest, 4, units)
    return (units * (CAP // 4)).astype(jnp.int32)


def with_spikes(values, key, source, target, blocks, factor):
    owner, partner = [(jnp.arange(values.shape[position]) // (values.shape[position] // blocks)).reshape([-1 if axis == position else 1 for axis in range(values.ndim)]) for position in (source, target)]
    chosen = jax.random.permutation(key, blocks)[partner]
    strong = (owner == chosen) | (owner == (partner + blocks // 2) % blocks)
    return jnp.where(strong, factor * values, values)


def block_scale(key, shape, shards, low, largest):
    level = 1.0
    for axis_at, shards_of in shards:
        heights = jax.random.uniform(jax.random.fold_in(jax.random.fold_in(key, 6), axis_at), (shards_of,), jnp.float32, low / len(shards), largest / len(shards))
        level = level * jnp.repeat(jnp.exp(heights), shape[axis_at] // shards_of).reshape((-1,) + (1,) * (len(shape) - 1 - axis_at))
    return level


def scatter_about(key, extent, deviation, reach, shards=(), dtype=jnp.bfloat16):
    values = jax.random.normal(key, extent, jnp.float32) * deviation
    if len(shards) > 0:
        values = block_scale(key, extent, shards, -0.22, 0.18) * values
    return jnp.clip(values, min=-reach, max=reach).astype(dtype)


def noise_with(rng, extent, width, bound, shards, heavy, kind=jnp.bfloat16):
    entries = width * jax.random.normal(rng, extent, jnp.float32)
    if shards:
        entries = entries * block_scale(rng, extent, shards, -0.22, 0.18)
    return jnp.clip(with_spikes(entries, jax.random.fold_in(rng, 3), *heavy), -bound, bound).astype(kind)


def setup_inputs(seed: int = 0) -> dict:
    arg_keys = jax.random.split(jax.random.key(seed), 13)
    return {
        "feat_sig": scatter_about(arg_keys[0], (TOKENS, C_SIG), 1.0, 6.0, ((0, 8), (1, 4))),
        "feat_cnx": scatter_about(arg_keys[1], (TOKENS, C_CNX), 1.0, 6.0, ((0, 8), (1, 4))),
        "cotangent": noise_with(arg_keys[2], (TOKENS, D), 1.0, 6.0, ((0, 8), (1, 4)), (0, 1, 8, 2.0)),
        "w_sig": scatter_about(arg_keys[3], (D, C_SIG), (C_SIG + C_CNX) ** -0.5, 0.09375, ((1, 4),)),
        "w_cnx": scatter_about(arg_keys[4], (D, C_CNX), (C_SIG + C_CNX) ** -0.5, 0.09375, ((1, 4),)),
        "lengths": draw_lengths(jax.random.fold_in(arg_keys[12], 71), 0),
        "enc_of": jax.vmap(lambda own: jax.random.permutation(own, N_DP))(jax.random.split(arg_keys[6], (N_DP * N_REP))).reshape((N_DP * N_REP, N_DP)).astype(jnp.int32),
        "owner_of": jax.vmap(lambda own: jax.random.permutation(own, N_DP))(jax.random.split(arg_keys[7], (N_DP * N_REP))).reshape((N_DP * N_REP, N_DP)).astype(jnp.int32),
        "pre_sig": scatter_about(arg_keys[8], (TOKENS, C_SIG), 1.0, 6.0, ((0, 8), (1, 4))),
        "pre_cnx": scatter_about(arg_keys[9], (TOKENS, C_CNX), 1.0, 6.0, ((0, 8), (1, 4))),
        "gain_sig": jnp.clip(jnp.exp(math.log(2.0) - 1.3862944 * jax.random.uniform(arg_keys[10], (C_SIG,), jnp.float32) ** block_scale(arg_keys[10], (C_SIG,), ((0, 4),), -0.2, 0.2)), 0.5, 2.0),
        "gain_cnx": jnp.clip(jnp.exp(math.log(2.0) - 1.3862944 * jax.random.uniform(arg_keys[11], (C_CNX,), jnp.float32) ** block_scale(arg_keys[11], (C_CNX,), ((0, 4),), -0.2, 0.2)), 0.5, 2.0),
    }


EPS = 1e-06

def live_mask(lengths):
    owners, slots = lengths.shape
    spots = lax.broadcasted_iota(jnp.int32, (owners, slots, CAP), 2)
    return (spots < lengths[:, :, None]).reshape(owners * slots * CAP, 1)

def route(grad_rows, enc_of, owner_of):
    owners, slots = enc_of.shape
    inverse = jnp.argsort(enc_of, axis=1).astype(jnp.int32)
    blocks = lax.broadcasted_iota(jnp.int32, (owners, slots), 0)
    enc_dev = blocks // N_REP
    rep_index = blocks % N_REP
    source_owner = (owner_of * N_REP + rep_index).astype(jnp.int32)
    source_slot = inverse[source_owner, enc_dev]
    flat = (source_owner * slots + source_slot).reshape(-1).astype(jnp.int32)
    cells = grad_rows.reshape(owners * slots, CAP, grad_rows.shape[1])
    return cells[flat].reshape(owners * slots * CAP, grad_rows.shape[1])

def norm_back(pre, grad_in, gain):
    feature_width = pre.shape[-1]
    row_height = pre.astype(jnp.float32)
    hidden_mean = lax.optimization_barrier(jnp.sum(row_height, axis=-1, keepdims=True)) / feature_width
    var_h = lax.optimization_barrier(jnp.sum(row_height * row_height, axis=-1, keepdims=True)) / feature_width - hidden_mean * hidden_mean
    inverse_deviation = lax.rsqrt(var_h + EPS)
    normalized_input = (row_height - hidden_mean) * inverse_deviation
    scaled_gradient = grad_in.astype(jnp.float32) * gain
    gradient_mean = lax.optimization_barrier(jnp.sum(scaled_gradient, axis=-1, keepdims=True)) / feature_width
    gradient_product_mean = lax.optimization_barrier(jnp.sum(scaled_gradient * normalized_input, axis=-1, keepdims=True)) / feature_width
    return (inverse_deviation * (scaled_gradient - gradient_mean - normalized_input * gradient_product_mean)).astype(jnp.bfloat16)

def blocked_norm(pre, grad_in, gain, owners):
    feature_width = pre.shape[1]
    pre_blocks = pre.reshape(owners, -1, feature_width)
    grad_blocks = grad_in.reshape(owners, -1, feature_width)
    result = lax.map(lambda pair: norm_back(pair[0], pair[1], gain), (pre_blocks, grad_blocks))
    return result.reshape(-1, feature_width)

def reference(feat_sig, feat_cnx, cotangent, w_sig, w_cnx, lengths, enc_of, owner_of, pre_sig, pre_cnx, gain_sig, gain_cnx):
    owners = lengths.shape[0]
    live = live_mask(lengths)
    masked = jnp.where(live, cotangent, jnp.zeros_like(cotangent))
    back_sig = jnp.dot(masked, w_sig, preferred_element_type=jnp.float32).astype(jnp.bfloat16)
    back_cnx = jnp.dot(masked, w_cnx, preferred_element_type=jnp.float32).astype(jnp.bfloat16)
    scale = 1.0 / math.sqrt(TOKENS)
    grad_w_sig = jnp.dot(masked.T, feat_sig, preferred_element_type=jnp.float32) * scale
    grad_w_cnx = jnp.dot(masked.T, feat_cnx, preferred_element_type=jnp.float32) * scale
    dy_sig = route(back_sig, enc_of, owner_of)
    dy_cnx = route(back_cnx, enc_of, owner_of)
    gradient_before_siglip = blocked_norm(pre_sig, dy_sig, gain_sig, owners)
    gradient_before_convnext = blocked_norm(pre_cnx, dy_cnx, gain_cnx, owners)
    return (grad_w_sig, grad_w_cnx, gradient_before_siglip, gradient_before_convnext)
```

```python
import functools
import math

import jax
import jax.numpy as jnp
from jax import lax
from jax.experimental import pallas as pl
from jax.experimental.pallas import tpu as pltpu
from jax.sharding import PartitionSpec as P

EPS = 1e-06
LANES = 128
GATHER_BYTES = 4 * 1024 * 1024
VMEM_BYTES = 58 * 1024 * 1024
MESH = pl.DeviceIdType.MESH


def row_statistics_pair(row_height, sum_h, sum_hh, feature_width):
    hidden_mean = sum_h[:, None] / feature_width
    var_h = sum_hh[:, None] / feature_width - hidden_mean * hidden_mean
    inverse_deviation = lax.rsqrt(var_h + EPS)
    return (hidden_mean, inverse_deviation, (row_height - hidden_mean) * inverse_deviation)


def partial_sum_shards(
    feat_sig,
    feat_cnx,
    cotangent,
    w_sig,
    w_cnx,
    lengths,
    enc_of,
    owner_of,
    pre_sig,
    pre_cnx,
    gain_sig,
    gain_cnx,
):
    slots = lengths.shape[1]
    rows = cotangent.shape[0]
    depth = rows // slots
    spots = lax.broadcasted_iota(jnp.int32, (slots, depth), 1)
    live = (spots < lengths[0][:, None]).reshape(rows, 1)
    masked = jnp.where(live, cotangent, jnp.zeros_like(cotangent))
    full_grad = lax.all_gather(masked, "enc", axis=1, tiled=True)
    back_sig = jnp.dot(full_grad, w_sig, preferred_element_type=jnp.float32).astype(jnp.bfloat16)
    back_cnx = jnp.dot(full_grad, w_cnx, preferred_element_type=jnp.float32).astype(jnp.bfloat16)
    inverse = jnp.argsort(enc_of[0])
    send_sig = jnp.take(back_sig.reshape(slots, depth, back_sig.shape[1]), inverse, axis=0)
    send_cnx = jnp.take(back_cnx.reshape(slots, depth, back_cnx.shape[1]), inverse, axis=0)
    recv_sig, recv_cnx = (
        lax.all_to_all(send_sig, "dp", split_axis=0, concat_axis=0, tiled=True),
        lax.all_to_all(send_cnx, "dp", split_axis=0, concat_axis=0, tiled=True),
    )
    sources = owner_of[0]
    dy_sig = jnp.take(recv_sig, sources, axis=0).reshape(rows, recv_sig.shape[2])
    dy_cnx = jnp.take(recv_cnx, sources, axis=0).reshape(rows, recv_cnx.shape[2])
    enc_count = lax.axis_size("enc")
    siglip_width = gain_sig.shape[0] * enc_count
    convnext_width = gain_cnx.shape[0] * enc_count
    siglip_height = pre_sig.astype(jnp.float32)
    convnext_height = pre_cnx.astype(jnp.float32)
    siglip_scaled_gradient = dy_sig.astype(jnp.float32) * gain_sig
    convnext_scaled_gradient = dy_cnx.astype(jnp.float32) * gain_cnx
    row_totals = lax.psum(
        (
            jnp.sum(siglip_height, axis=1),
            jnp.sum(siglip_height * siglip_height, axis=1),
            jnp.sum(convnext_height, axis=1),
            jnp.sum(convnext_height * convnext_height, axis=1),
        ),
        "enc",
    )
    siglip_mean, siglip_inverse_deviation, siglip_normalized = row_statistics_pair(
        siglip_height, row_totals[0], row_totals[1], siglip_width
    )
    convnext_mean, convnext_inverse_deviation, convnext_normalized = row_statistics_pair(
        convnext_height, row_totals[2], row_totals[3], convnext_width
    )
    later = lax.psum(
        (
            jnp.sum(siglip_scaled_gradient, axis=1),
            jnp.sum(siglip_scaled_gradient * siglip_normalized, axis=1),
            jnp.sum(convnext_scaled_gradient, axis=1),
            jnp.sum(convnext_scaled_gradient * convnext_normalized, axis=1),
        ),
        "enc",
    )
    siglip_gradient_mean = later[0][:, None] / siglip_width
    siglip_product_mean = later[1][:, None] / siglip_width
    convnext_gradient_mean = later[2][:, None] / convnext_width
    convnext_product_mean = later[3][:, None] / convnext_width
    gradient_before_siglip = (
        siglip_inverse_deviation
        * (siglip_scaled_gradient - siglip_gradient_mean - siglip_normalized * siglip_product_mean)
    ).astype(jnp.bfloat16)
    gradient_before_convnext = (
        convnext_inverse_deviation
        * (
            convnext_scaled_gradient
            - convnext_gradient_mean
            - convnext_normalized * convnext_product_mean
        )
    ).astype(jnp.bfloat16)
    dp_count = lax.axis_size("dp")
    rep_count = lax.axis_size("rep")
    scale = 1.0 / math.sqrt(rows * dp_count * rep_count)
    split = feat_sig.shape[1]
    features = jnp.concatenate([feat_sig, feat_cnx], axis=1)
    summed = lax.psum_scatter(
        lax.dot_general(
            full_grad, features, (((0,), (0,)), ((), ())), preferred_element_type=jnp.float32
        ),
        ("dp", "rep"),
        scatter_dimension=0,
        tiled=True,
    )
    summed = summed * scale
    return (summed[:, :split], summed[:, split:], gradient_before_siglip, gradient_before_convnext)


def round_up(width):
    return -(-width // LANES) * LANES


def fused_kernel(
    sizes,
    lengths_hbm,
    enc_of_hbm,
    owner_of_hbm,
    cot_hbm,
    fs_hbm,
    fc_hbm,
    ps_hbm,
    pc_hbm,
    gs_hbm,
    gc_hbm,
    ws_hbm,
    wc_hbm,
    gws_ref,
    gwc_ref,
    os_ref,
    oc_ref,
    len_s,
    enc_s,
    own_s,
    cot_v,
    fs_v,
    fc_v,
    ps_v,
    pc_v,
    gs_v,
    gc_v,
    ws_v,
    wc_v,
    fg,
    fa,
    cc,
    sb,
    rb,
    st1,
    st2,
    joint,
    height,
    dy,
    local_sem,
    w_sem,
    fg_send,
    fg_recv,
    fa_send,
    fa_recv,
    fwd_send,
    cc_send,
    cc_recv,
    rb_send,
    rb_recv,
    st1_send,
    st1_recv,
    st2_send,
    st2_recv,
):
    n_enc, n_dp, n_rep, slots, depth = sizes
    rows = slots * depth
    e, d, r = lax.axis_index("enc"), lax.axis_index("dp"), lax.axis_index("rep")
    chunk = cot_v.shape[1]
    cs, cn = fs_v.shape[1], fc_v.shape[1]
    lo = round_up(cs)
    block = cc.shape[2]
    per = chunk // block
    width_s, width_c = cs * n_enc, cn * n_enc
    b = d * n_rep + r
    enc_peers = [lax.rem(e + k, n_enc) for k in range(1, n_enc)]
    dp_peers = [lax.rem(d + k, n_dp) for k in range(1, n_dp)]
    partner = 1 - r

    barrier = pltpu.get_barrier_semaphore()
    for p in enc_peers:
        pl.semaphore_signal(barrier, inc=1, device_id=(p, d, r), device_id_type=MESH)
    for q in dp_peers:
        for s in range(n_rep):
            pl.semaphore_signal(barrier, inc=1, device_id=(e, q, s), device_id_type=MESH)
    pl.semaphore_signal(barrier, inc=1, device_id=(e, d, partner), device_id_type=MESH)

    pairs = (
        (lengths_hbm, len_s),
        (enc_of_hbm, enc_s),
        (owner_of_hbm, own_s),
        (cot_hbm, cot_v),
        (fs_hbm, fs_v),
        (fc_hbm, fc_v),
        (ps_hbm, ps_v),
        (pc_hbm, pc_v),
        (gs_hbm, gs_v),
        (gc_hbm, gc_v),
    )
    loads = [
        pltpu.make_async_copy(source, target, local_sem.at[i])
        for i, (source, target) in enumerate(pairs)
    ]
    for load in loads:
        load.start()
    w_loads = []
    for k in range(n_enc):
        p = lax.rem(e + k, n_enc)
        at = pl.ds(pl.multiple_of(p * chunk, chunk), chunk)
        pair = (
            pltpu.make_async_copy(ws_hbm.at[:, at], ws_v.at[:, at], w_sem.at[2 * k]),
            pltpu.make_async_copy(wc_hbm.at[at], wc_v.at[at], w_sem.at[2 * k + 1]),
        )
        for load in pair:
            load.start()
        w_loads.append(pair)

    for i in range(4):
        loads[i].wait()
    row = lax.broadcasted_iota(jnp.int32, (rows, rows), 0)
    col = lax.broadcasted_iota(jnp.int32, (rows, rows), 1)
    same_spot = lax.rem(row, depth) == lax.rem(col, depth)
    pick = jnp.zeros((rows, rows), jnp.float32)
    for j in range(slots):
        taken = (col // depth == j) & (row // depth == enc_s[0, j])
        taken = taken & same_spot & (lax.rem(col, depth) < len_s[0, j])
        pick = jnp.where(taken, 1.0, pick)
    pick = pick.astype(jnp.bfloat16)
    mine = jnp.dot(pick, cot_v[...], preferred_element_type=jnp.float32).astype(jnp.bfloat16)
    fg[e] = mine

    pl.semaphore_wait(barrier, n_enc - 1 + n_dp * n_rep - 1)

    sent = []

    def send(src, dst, send_sem, recv_sem, device):
        copy = pltpu.make_async_remote_copy(
            src_ref=src,
            dst_ref=dst,
            send_sem=send_sem,
            recv_sem=recv_sem,
            device_id=device,
            device_id_type=MESH,
        )
        copy.start()
        sent.append(copy)

    def arrived(dst, recv_sem, device):
        pltpu.make_async_remote_copy(
            src_ref=dst,
            dst_ref=dst,
            send_sem=recv_sem,
            recv_sem=recv_sem,
            device_id=device,
            device_id_type=MESH,
        ).wait_recv()

    for k, p in enumerate(enc_peers):
        send(fg.at[e], fg.at[e], fg_send.at[k], fg_recv.at[e], (p, d, r))

    loads[4].wait()
    loads[5].wait()
    fa[b] = jnp.zeros_like(fa[b])
    fa[b, :, 0:cs] = jnp.dot(pick, fs_v[...], preferred_element_type=jnp.float32).astype(
        jnp.bfloat16
    )
    fa[b, :, lo : lo + cn] = jnp.dot(
        pick, fc_v[...], preferred_element_type=jnp.float32
    ).astype(jnp.bfloat16)
    for k, q in enumerate(dp_peers):
        send(fa.at[b], fa.at[b], fa_send.at[k], fa_recv.at[b], (e, q, r))
    send(fa.at[b], fa.at[b], fa_send.at[n_dp - 1], fa_recv.at[b], (e, d, partner))

    loads[6].wait()
    loads[7].wait()
    height[...] = jnp.zeros_like(height)
    height[:, 0:cs] = ps_v[...].astype(jnp.float32)
    height[:, lo : lo + cn] = pc_v[...].astype(jnp.float32)
    h_s, h_c = height[:, 0:lo], height[:, lo:]
    lane = lax.broadcasted_iota(jnp.int32, (rows, LANES), 1)

    def four(values):
        sums = [jnp.sum(v, axis=1, keepdims=True) for v in values]
        packed = jnp.zeros((rows, LANES), jnp.float32)
        for i, total in enumerate(sums):
            packed = jnp.where(lane == i, total, packed)
        return packed

    st1[e] = four((h_s, h_s * h_s, h_c, h_c * h_c))
    for k, p in enumerate(enc_peers):
        send(st1.at[e], st1.at[e], st1_send.at[k], st1_recv.at[e], (p, d, r))

    acc_s = jnp.zeros((rows, cs), jnp.float32)
    acc_c = jnp.zeros((rows, cn), jnp.float32)
    for k in range(n_enc):
        p = lax.rem(e + k, n_enc)
        at = pl.ds(pl.multiple_of(p * chunk, chunk), chunk)
        for load in w_loads[k]:
            load.wait()
        if k > 0:
            arrived(fg.at[p], fg_recv.at[p], (p, d, r))
        part = fg[p]
        acc_s += lax.dot_general(
            part, ws_v[:, at], (((1,), (1,)), ((), ())), preferred_element_type=jnp.float32
        )
        acc_c += jnp.dot(part, wc_v[at, :], preferred_element_type=jnp.float32)
    joint[...] = jnp.zeros_like(joint)
    joint[:, 0:cs] = acc_s
    joint[:, lo : lo + cn] = acc_c
    for i in range(slots):
        sb[i] = joint[i * depth : (i + 1) * depth, :].astype(jnp.bfloat16)
    rb[d] = sb[d]
    for k, q in enumerate(dp_peers):
        send(sb.at[q], rb.at[d], rb_send.at[k], rb_recv.at[d], (e, q, r))

    def my_block(q, s):
        first = q * n_rep + s
        return fg.at[first // per, :, pl.ds(pl.multiple_of(lax.rem(first, per) * block, block), block)]

    cc[b] = my_block(d, r)[...]
    count = 0
    for q in dp_peers:
        for s in range(n_rep):
            send(my_block(q, s), cc.at[b], cc_send.at[count], cc_recv.at[b], (e, q, s))
            count += 1
    send(my_block(d, partner), cc.at[b], cc_send.at[count], cc_recv.at[b], (e, d, partner))

    for k, q in enumerate(dp_peers):
        at = q * n_rep + r
        arrived(fa.at[at], fa_recv.at[at], (e, q, r))
        send(fa.at[at], fa.at[at], fwd_send.at[k], fa_recv.at[at], (e, d, partner))

    for p in enc_peers:
        arrived(st1.at[p], st1_recv.at[p], (p, d, r))
    total = st1[0]
    for i in range(1, n_enc):
        total += st1[i]

    def normalize(h, sum_h, sum_hh, width):
        mean = sum_h / width
        rstd = lax.rsqrt(sum_hh / width - mean * mean + EPS)
        return rstd, (h - mean) * rstd

    rstd_s, xhat_s = normalize(h_s, total[:, 0:1], total[:, 1:2], width_s)
    rstd_c, xhat_c = normalize(h_c, total[:, 2:3], total[:, 3:4], width_c)

    for q in dp_peers:
        arrived(rb.at[q], rb_recv.at[q], (e, q, r))
    pieces = [rb[o].astype(jnp.float32) for o in range(n_dp)]
    for i in range(slots):
        chosen = pieces[0]
        for o in range(1, n_dp):
            chosen = jnp.where(own_s[0, i] == o, pieces[o], chosen)
        dy[i * depth : (i + 1) * depth, :] = chosen
    loads[8].wait()
    loads[9].wait()
    joint[...] = jnp.zeros_like(joint)
    joint[:, 0:cs] = dy[:, 0:cs] * gs_v[...]
    joint[:, lo : lo + cn] = dy[:, lo : lo + cn] * gc_v[...]
    gy_s, gy_c = joint[:, 0:lo], joint[:, lo:]
    st2[e] = four((gy_s, gy_s * xhat_s, gy_c, gy_c * xhat_c))
    for k, p in enumerate(enc_peers):
        send(st2.at[e], st2.at[e], st2_send.at[k], st2_recv.at[e], (p, d, r))

    for q in dp_peers:
        for s in range(n_rep):
            at = q * n_rep + s
            arrived(cc.at[at], cc_recv.at[at], (e, q, s))
        other = q * n_rep + partner
        arrived(fa.at[other], fa_recv.at[other], (e, d, partner))
    beside = d * n_rep + partner
    arrived(cc.at[beside], cc_recv.at[beside], (e, d, partner))
    arrived(fa.at[beside], fa_recv.at[beside], (e, d, partner))
    tokens = n_dp * n_rep * rows
    scale = 1.0 / math.sqrt(tokens)
    cot_all = cc[...].reshape(tokens, block)
    over_rows = (((0,), (0,)), ((), ()))
    gws_ref[...] = (
        lax.dot_general(
            fa[:, :, 0:lo].reshape(tokens, lo),
            cot_all,
            over_rows,
            preferred_element_type=jnp.float32,
        )[0:cs, :]
        * scale
    )
    gwc_ref[...] = (
        lax.dot_general(
            cot_all,
            fa[:, :, lo:].reshape(tokens, fa.shape[2] - lo),
            over_rows,
            preferred_element_type=jnp.float32,
        )[:, 0:cn]
        * scale
    )

    for p in enc_peers:
        arrived(st2.at[p], st2_recv.at[p], (p, d, r))
    later = st2[0]
    for i in range(1, n_enc):
        later += st2[i]
    mean_s, prod_s = later[:, 0:1] / width_s, later[:, 1:2] / width_s
    mean_c, prod_c = later[:, 2:3] / width_c, later[:, 3:4] / width_c
    os_ref[...] = (rstd_s * (gy_s - mean_s - xhat_s * prod_s))[:, 0:cs].astype(os_ref.dtype)
    oc_ref[...] = (rstd_c * (gy_c - mean_c - xhat_c * prod_c))[:, 0:cn].astype(oc_ref.dtype)

    for copy in sent:
        copy.wait_send()


def gather_shards(
    feat_sig,
    feat_cnx,
    cotangent,
    w_sig,
    w_cnx,
    lengths,
    enc_of,
    owner_of,
    pre_sig,
    pre_cnx,
    gain_sig,
    gain_cnx,
):
    n_enc, n_dp, n_rep = (lax.axis_size(axis) for axis in ("enc", "dp", "rep"))
    slots = lengths.shape[1]
    rows, chunk = cotangent.shape
    depth = rows // slots
    cs, cn = feat_sig.shape[1], feat_cnx.shape[1]
    whole = w_sig.shape[0]
    owners = n_dp * n_rep
    block = whole // owners
    joint = round_up(cs) + round_up(cn)
    bf16, f32 = jnp.bfloat16, jnp.float32
    dma = pltpu.SemaphoreType.DMA
    scratch = [
        pltpu.SMEM((1, slots), jnp.int32),
        pltpu.SMEM((1, slots), jnp.int32),
        pltpu.SMEM((1, slots), jnp.int32),
        pltpu.VMEM((rows, chunk), bf16),
        pltpu.VMEM((rows, cs), bf16),
        pltpu.VMEM((rows, cn), bf16),
        pltpu.VMEM((rows, cs), bf16),
        pltpu.VMEM((rows, cn), bf16),
        pltpu.VMEM((1, cs), f32),
        pltpu.VMEM((1, cn), f32),
        pltpu.VMEM((cs, whole), bf16),
        pltpu.VMEM((whole, cn), bf16),
        pltpu.VMEM((n_enc, rows, chunk), bf16),
        pltpu.VMEM((owners, rows, joint), bf16),
        pltpu.VMEM((owners, rows, block), bf16),
        pltpu.VMEM((n_dp, depth, joint), bf16),
        pltpu.VMEM((n_dp, depth, joint), bf16),
        pltpu.VMEM((n_enc, rows, LANES), f32),
        pltpu.VMEM((n_enc, rows, LANES), f32),
        pltpu.VMEM((rows, joint), f32),
        pltpu.VMEM((rows, joint), f32),
        pltpu.VMEM((rows, joint), f32),
        dma((10,)),
        dma((2 * n_enc,)),
        dma((n_enc,)),
        dma((n_enc,)),
        dma((n_dp,)),
        dma((owners,)),
        dma((n_dp,)),
        dma((owners,)),
        dma((owners,)),
        dma((n_dp,)),
        dma((n_dp,)),
        dma((n_enc,)),
        dma((n_enc,)),
        dma((n_enc,)),
        dma((n_enc,)),
    ]
    anywhere, vmem = pl.BlockSpec(memory_space=pl.ANY), pl.BlockSpec(memory_space=pltpu.VMEM)
    grad_w_sig, *rest = pl.pallas_call(
        functools.partial(fused_kernel, (n_enc, n_dp, n_rep, slots, depth)),
        out_shape=(
            jax.ShapeDtypeStruct((cs, block), f32),
            jax.ShapeDtypeStruct((block, cn), f32),
            jax.ShapeDtypeStruct((rows, cs), bf16),
            jax.ShapeDtypeStruct((rows, cn), bf16),
        ),
        in_specs=[anywhere] * 12,
        out_specs=(vmem,) * 4,
        scratch_shapes=scratch,
        compiler_params=pltpu.CompilerParams(
            collective_id=0, has_side_effects=True, vmem_limit_bytes=VMEM_BYTES
        ),
        cost_estimate=pl.CostEstimate(
            flops=2 * rows * whole * (cs + cn) * 2,
            bytes_accessed=2 * whole * (cs + cn) + 4 * block * (cs + cn),
            transcendentals=2 * rows,
        ),
    )(
        lengths,
        enc_of,
        owner_of,
        cotangent,
        feat_sig,
        feat_cnx,
        pre_sig,
        pre_cnx,
        gain_sig.reshape(1, cs),
        gain_cnx.reshape(1, cn),
        w_sig.T,
        w_cnx,
    )
    return (grad_w_sig.T, *rest)


def shards(feat_sig, feat_cnx, cotangent, w_sig, *others):
    n_enc, n_dp, n_rep = (lax.axis_size(axis) for axis in ("enc", "dp", "rep"))
    rows, chunk = cotangent.shape
    owners = n_dp * n_rep
    whole = w_sig.shape[0]
    gathered = owners * rows * (feat_sig.shape[1] + feat_cnx.shape[1]) * 2
    fits = gathered <= GATHER_BYTES and n_rep == 2 and rows % 16 == 0
    fits = fits and others[1].shape[1] == n_dp and whole % (owners * LANES) == 0
    fits = fits and chunk % (whole // owners) == 0
    form = gather_shards if fits else partial_sum_shards
    return form(feat_sig, feat_cnx, cotangent, w_sig, *others)


def solution(mesh):
    in_specs = (
        P(("dp", "rep"), "enc"),
        P(("dp", "rep"), "enc"),
        P(("dp", "rep"), "enc"),
        P(None, "enc"),
        P(None, "enc"),
        P(("dp", "rep"), None),
        P(("dp", "rep"), None),
        P(("dp", "rep"), None),
        P(("dp", "rep"), "enc"),
        P(("dp", "rep"), "enc"),
        P("enc"),
        P("enc"),
    )
    out_specs = (
        P(("dp", "rep"), "enc"),
        P(("dp", "rep"), "enc"),
        P(("dp", "rep"), "enc"),
        P(("dp", "rep"), "enc"),
    )
    return jax.shard_map(shards, mesh=mesh, in_specs=in_specs, out_specs=out_specs, check_vma=False)
```

```python
import functools
import math

import jax
import jax.numpy as jnp
from jax import lax
from jax.experimental import pallas as pl
from jax.experimental.pallas import tpu as pltpu
from jax.sharding import PartitionSpec as P

EPS = 1e-06
LANES = 128
GATHER_BYTES = 4 * 1024 * 1024
VMEM_BYTES = 58 * 1024 * 1024
MESH = pl.DeviceIdType.MESH


def row_statistics_pair(row_height, sum_h, sum_hh, feature_width):
    hidden_mean = sum_h[:, None] / feature_width
    var_h = sum_hh[:, None] / feature_width - hidden_mean * hidden_mean
    inverse_deviation = lax.rsqrt(var_h + EPS)
    return (hidden_mean, inverse_deviation, (row_height - hidden_mean) * inverse_deviation)


def partial_sum_shards(
    feat_sig,
    feat_cnx,
    cotangent,
    w_sig,
    w_cnx,
    lengths,
    enc_of,
    owner_of,
    pre_sig,
    pre_cnx,
    gain_sig,
    gain_cnx,
):
    slots = lengths.shape[1]
    rows = cotangent.shape[0]
    depth = rows // slots
    spots = lax.broadcasted_iota(jnp.int32, (slots, depth), 1)
    live = (spots < lengths[0][:, None]).reshape(rows, 1)
    masked = jnp.where(live, cotangent, jnp.zeros_like(cotangent))
    full_grad = lax.all_gather(masked, "enc", axis=1, tiled=True)
    back_sig = jnp.dot(full_grad, w_sig, preferred_element_type=jnp.float32).astype(jnp.bfloat16)
    back_cnx = jnp.dot(full_grad, w_cnx, preferred_element_type=jnp.float32).astype(jnp.bfloat16)
    inverse = jnp.argsort(enc_of[0])
    send_sig = jnp.take(back_sig.reshape(slots, depth, back_sig.shape[1]), inverse, axis=0)
    send_cnx = jnp.take(back_cnx.reshape(slots, depth, back_cnx.shape[1]), inverse, axis=0)
    recv_sig, recv_cnx = (
        lax.all_to_all(send_sig, "dp", split_axis=0, concat_axis=0, tiled=True),
        lax.all_to_all(send_cnx, "dp", split_axis=0, concat_axis=0, tiled=True),
    )
    sources = owner_of[0]
    dy_sig = jnp.take(recv_sig, sources, axis=0).reshape(rows, recv_sig.shape[2])
    dy_cnx = jnp.take(recv_cnx, sources, axis=0).reshape(rows, recv_cnx.shape[2])
    enc_count = lax.axis_size("enc")
    siglip_width = gain_sig.shape[0] * enc_count
    convnext_width = gain_cnx.shape[0] * enc_count
    siglip_height = pre_sig.astype(jnp.float32)
    convnext_height = pre_cnx.astype(jnp.float32)
    siglip_scaled_gradient = dy_sig.astype(jnp.float32) * gain_sig
    convnext_scaled_gradient = dy_cnx.astype(jnp.float32) * gain_cnx
    row_totals = lax.psum(
        (
            jnp.sum(siglip_height, axis=1),
            jnp.sum(siglip_height * siglip_height, axis=1),
            jnp.sum(convnext_height, axis=1),
            jnp.sum(convnext_height * convnext_height, axis=1),
        ),
        "enc",
    )
    siglip_mean, siglip_inverse_deviation, siglip_normalized = row_statistics_pair(
        siglip_height, row_totals[0], row_totals[1], siglip_width
    )
    convnext_mean, convnext_inverse_deviation, convnext_normalized = row_statistics_pair(
        convnext_height, row_totals[2], row_totals[3], convnext_width
    )
    later = lax.psum(
        (
            jnp.sum(siglip_scaled_gradient, axis=1),
            jnp.sum(siglip_scaled_gradient * siglip_normalized, axis=1),
            jnp.sum(convnext_scaled_gradient, axis=1),
            jnp.sum(convnext_scaled_gradient * convnext_normalized, axis=1),
        ),
        "enc",
    )
    siglip_gradient_mean = later[0][:, None] / siglip_width
    siglip_product_mean = later[1][:, None] / siglip_width
    convnext_gradient_mean = later[2][:, None] / convnext_width
    convnext_product_mean = later[3][:, None] / convnext_width
    gradient_before_siglip = (
        siglip_inverse_deviation
        * (siglip_scaled_gradient - siglip_gradient_mean - siglip_normalized * siglip_product_mean)
    ).astype(jnp.bfloat16)
    gradient_before_convnext = (
        convnext_inverse_deviation
        * (
            convnext_scaled_gradient
            - convnext_gradient_mean
            - convnext_normalized * convnext_product_mean
        )
    ).astype(jnp.bfloat16)
    dp_count = lax.axis_size("dp")
    rep_count = lax.axis_size("rep")
    scale = 1.0 / math.sqrt(rows * dp_count * rep_count)
    split = feat_sig.shape[1]
    features = jnp.concatenate([feat_sig, feat_cnx], axis=1)
    summed = lax.psum_scatter(
        lax.dot_general(
            full_grad, features, (((0,), (0,)), ((), ())), preferred_element_type=jnp.float32
        ),
        ("dp", "rep"),
        scatter_dimension=0,
        tiled=True,
    )
    summed = summed * scale
    return (summed[:, :split], summed[:, split:], gradient_before_siglip, gradient_before_convnext)


def round_up(width):
    return -(-width // LANES) * LANES


def fused_kernel(
    sizes,
    lengths_hbm,
    enc_of_hbm,
    owner_of_hbm,
    cot_hbm,
    fs_hbm,
    fc_hbm,
    ps_hbm,
    pc_hbm,
    gs_hbm,
    gc_hbm,
    ws_hbm,
    wc_hbm,
    fa,
    cc,
    os_ref,
    oc_ref,
    len_s,
    enc_s,
    own_s,
    cot_v,
    fs_v,
    fc_v,
    ps_v,
    pc_v,
    gs_v,
    gc_v,
    ws_v,
    wc_v,
    fg,
    sb,
    rb,
    st1,
    st2,
    joint,
    height,
    dy,
    local_sem,
    w_sem,
    fg_send,
    fg_recv,
    fa_send,
    fa_recv,
    fwd_send,
    cc_send,
    cc_recv,
    rb_send,
    rb_recv,
    st1_send,
    st1_recv,
    st2_send,
    st2_recv,
):
    n_enc, n_dp, n_rep, slots, depth = sizes
    rows = slots * depth
    e, d, r = lax.axis_index("enc"), lax.axis_index("dp"), lax.axis_index("rep")
    chunk = cot_v.shape[1]
    cs, cn = fs_v.shape[1], fc_v.shape[1]
    lo = round_up(cs)
    block = cc.shape[2]
    per = chunk // block
    width_s, width_c = cs * n_enc, cn * n_enc
    b = d * n_rep + r
    enc_peers = [lax.rem(e + k, n_enc) for k in range(1, n_enc)]
    dp_peers = [lax.rem(d + k, n_dp) for k in range(1, n_dp)]
    partner = 1 - r

    barrier = pltpu.get_barrier_semaphore()
    for p in enc_peers:
        pl.semaphore_signal(barrier, inc=1, device_id=(p, d, r), device_id_type=MESH)
    for q in dp_peers:
        for s in range(n_rep):
            pl.semaphore_signal(barrier, inc=1, device_id=(e, q, s), device_id_type=MESH)
    pl.semaphore_signal(barrier, inc=1, device_id=(e, d, partner), device_id_type=MESH)

    pairs = (
        (lengths_hbm, len_s),
        (enc_of_hbm, enc_s),
        (owner_of_hbm, own_s),
        (cot_hbm, cot_v),
        (fs_hbm, fs_v),
        (fc_hbm, fc_v),
        (ps_hbm, ps_v),
        (pc_hbm, pc_v),
        (gs_hbm, gs_v),
        (gc_hbm, gc_v),
    )
    loads = [
        pltpu.make_async_copy(source, target, local_sem.at[i])
        for i, (source, target) in enumerate(pairs)
    ]
    for load in loads:
        load.start()
    w_loads = []
    for k in range(n_enc):
        p = lax.rem(e + k, n_enc)
        at = pl.ds(pl.multiple_of(p * chunk, chunk), chunk)
        pair = (
            pltpu.make_async_copy(ws_hbm.at[:, at], ws_v.at[:, at], w_sem.at[2 * k]),
            pltpu.make_async_copy(wc_hbm.at[at], wc_v.at[at], w_sem.at[2 * k + 1]),
        )
        for load in pair:
            load.start()
        w_loads.append(pair)

    for i in range(4):
        loads[i].wait()
    row = lax.broadcasted_iota(jnp.int32, (rows, rows), 0)
    col = lax.broadcasted_iota(jnp.int32, (rows, rows), 1)
    same_spot = lax.rem(row, depth) == lax.rem(col, depth)
    pick = jnp.zeros((rows, rows), jnp.float32)
    for j in range(slots):
        taken = (col // depth == j) & (row // depth == enc_s[0, j])
        taken = taken & same_spot & (lax.rem(col, depth) < len_s[0, j])
        pick = jnp.where(taken, 1.0, pick)
    pick = pick.astype(jnp.bfloat16)
    mine = jnp.dot(pick, cot_v[...], preferred_element_type=jnp.float32).astype(jnp.bfloat16)
    fg[e] = mine

    pl.semaphore_wait(barrier, n_enc - 1 + n_dp * n_rep - 1)

    sent = []

    def send(src, dst, send_sem, recv_sem, device):
        copy = pltpu.make_async_remote_copy(
            src_ref=src,
            dst_ref=dst,
            send_sem=send_sem,
            recv_sem=recv_sem,
            device_id=device,
            device_id_type=MESH,
        )
        copy.start()
        sent.append(copy)

    def arrived(dst, recv_sem, device):
        pltpu.make_async_remote_copy(
            src_ref=dst,
            dst_ref=dst,
            send_sem=recv_sem,
            recv_sem=recv_sem,
            device_id=device,
            device_id_type=MESH,
        ).wait_recv()

    for k, p in enumerate(enc_peers):
        send(fg.at[e], fg.at[e], fg_send.at[k], fg_recv.at[e], (p, d, r))

    loads[4].wait()
    loads[5].wait()
    fa[b] = jnp.zeros_like(fa[b])
    fa[b, :, 0:cs] = jnp.dot(pick, fs_v[...], preferred_element_type=jnp.float32).astype(
        jnp.bfloat16
    )
    fa[b, :, lo : lo + cn] = jnp.dot(
        pick, fc_v[...], preferred_element_type=jnp.float32
    ).astype(jnp.bfloat16)
    for k, q in enumerate(dp_peers):
        send(fa.at[b], fa.at[b], fa_send.at[k], fa_recv.at[b], (e, q, r))
    send(fa.at[b], fa.at[b], fa_send.at[n_dp - 1], fa_recv.at[b], (e, d, partner))

    loads[6].wait()
    loads[7].wait()
    height[...] = jnp.zeros_like(height)
    height[:, 0:cs] = ps_v[...].astype(jnp.float32)
    height[:, lo : lo + cn] = pc_v[...].astype(jnp.float32)
    h_s, h_c = height[:, 0:lo], height[:, lo:]
    lane = lax.broadcasted_iota(jnp.int32, (rows, LANES), 1)

    def four(values):
        sums = [jnp.sum(v, axis=1, keepdims=True) for v in values]
        packed = jnp.zeros((rows, LANES), jnp.float32)
        for i, total in enumerate(sums):
            packed = jnp.where(lane == i, total, packed)
        return packed

    st1[e] = four((h_s, h_s * h_s, h_c, h_c * h_c))
    for k, p in enumerate(enc_peers):
        send(st1.at[e], st1.at[e], st1_send.at[k], st1_recv.at[e], (p, d, r))

    acc_s = jnp.zeros((rows, cs), jnp.float32)
    acc_c = jnp.zeros((rows, cn), jnp.float32)
    for k in range(n_enc):
        p = lax.rem(e + k, n_enc)
        at = pl.ds(pl.multiple_of(p * chunk, chunk), chunk)
        for load in w_loads[k]:
            load.wait()
        if k > 0:
            arrived(fg.at[p], fg_recv.at[p], (p, d, r))
        part = fg[p]
        acc_s += lax.dot_general(
            part, ws_v[:, at], (((1,), (1,)), ((), ())), preferred_element_type=jnp.float32
        )
        acc_c += jnp.dot(part, wc_v[at, :], preferred_element_type=jnp.float32)
    joint[...] = jnp.zeros_like(joint)
    joint[:, 0:cs] = acc_s
    joint[:, lo : lo + cn] = acc_c
    for i in range(slots):
        sb[i] = joint[i * depth : (i + 1) * depth, :].astype(jnp.bfloat16)
    rb[d] = sb[d]
    for k, q in enumerate(dp_peers):
        send(sb.at[q], rb.at[d], rb_send.at[k], rb_recv.at[d], (e, q, r))

    def my_block(q, s):
        first = q * n_rep + s
        return fg.at[first // per, :, pl.ds(pl.multiple_of(lax.rem(first, per) * block, block), block)]

    cc[b] = my_block(d, r)[...]
    count = 0
    for q in dp_peers:
        for s in range(n_rep):
            send(my_block(q, s), cc.at[b], cc_send.at[count], cc_recv.at[b], (e, q, s))
            count += 1
    send(my_block(d, partner), cc.at[b], cc_send.at[count], cc_recv.at[b], (e, d, partner))

    for p in enc_peers:
        arrived(st1.at[p], st1_recv.at[p], (p, d, r))
    total = st1[0]
    for i in range(1, n_enc):
        total += st1[i]

    def normalize(h, sum_h, sum_hh, width):
        mean = sum_h / width
        rstd = lax.rsqrt(sum_hh / width - mean * mean + EPS)
        return rstd, (h - mean) * rstd

    rstd_s, xhat_s = normalize(h_s, total[:, 0:1], total[:, 1:2], width_s)
    rstd_c, xhat_c = normalize(h_c, total[:, 2:3], total[:, 3:4], width_c)

    for k, q in enumerate(dp_peers):
        at = q * n_rep + r
        arrived(fa.at[at], fa_recv.at[at], (e, q, r))
        send(fa.at[at], fa.at[at], fwd_send.at[k], fa_recv.at[at], (e, d, partner))

    for q in dp_peers:
        arrived(rb.at[q], rb_recv.at[q], (e, q, r))
    pieces = [rb[o].astype(jnp.float32) for o in range(n_dp)]
    for i in range(slots):
        chosen = pieces[0]
        for o in range(1, n_dp):
            chosen = jnp.where(own_s[0, i] == o, pieces[o], chosen)
        dy[i * depth : (i + 1) * depth, :] = chosen
    loads[8].wait()
    loads[9].wait()
    joint[...] = jnp.zeros_like(joint)
    joint[:, 0:cs] = dy[:, 0:cs] * gs_v[...].reshape(1, cs)
    joint[:, lo : lo + cn] = dy[:, lo : lo + cn] * gc_v[...].reshape(1, cn)
    gy_s, gy_c = joint[:, 0:lo], joint[:, lo:]
    st2[e] = four((gy_s, gy_s * xhat_s, gy_c, gy_c * xhat_c))
    for k, p in enumerate(enc_peers):
        send(st2.at[e], st2.at[e], st2_send.at[k], st2_recv.at[e], (p, d, r))

    for p in enc_peers:
        arrived(st2.at[p], st2_recv.at[p], (p, d, r))
    later = st2[0]
    for i in range(1, n_enc):
        later += st2[i]
    mean_s, prod_s = later[:, 0:1] / width_s, later[:, 1:2] / width_s
    mean_c, prod_c = later[:, 2:3] / width_c, later[:, 3:4] / width_c
    os_ref[...] = (rstd_s * (gy_s - mean_s - xhat_s * prod_s))[:, 0:cs].astype(os_ref.dtype)
    oc_ref[...] = (rstd_c * (gy_c - mean_c - xhat_c * prod_c))[:, 0:cn].astype(oc_ref.dtype)

    for q in dp_peers:
        for s in range(n_rep):
            at = q * n_rep + s
            arrived(cc.at[at], cc_recv.at[at], (e, q, s))
        other = q * n_rep + partner
        arrived(fa.at[other], fa_recv.at[other], (e, d, partner))
    beside = d * n_rep + partner
    arrived(cc.at[beside], cc_recv.at[beside], (e, d, partner))
    arrived(fa.at[beside], fa_recv.at[beside], (e, d, partner))

    for copy in sent:
        copy.wait_send()


def weight_kernel(
    scale, fa, cc, os_v, oc_v, gws_hbm, gwc_hbm, os_hbm, oc_hbm, gws_v, gwc_v, out_sem
):
    tokens = cc.shape[0] * cc.shape[1]
    cs, cn = gws_v.shape[0], gwc_v.shape[1]
    lo = round_up(cs)
    stores = [
        pltpu.make_async_copy(os_v, os_hbm, out_sem.at[0]),
        pltpu.make_async_copy(oc_v, oc_hbm, out_sem.at[1]),
        pltpu.make_async_copy(gws_v, gws_hbm, out_sem.at[2]),
        pltpu.make_async_copy(gwc_v, gwc_hbm, out_sem.at[3]),
    ]
    stores[0].start()
    stores[1].start()
    cot_all = cc[...].reshape(tokens, cc.shape[2])
    over_rows = (((0,), (0,)), ((), ()))
    gws_v[...] = (
        lax.dot_general(
            fa[:, :, 0:lo].reshape(tokens, lo),
            cot_all,
            over_rows,
            preferred_element_type=jnp.float32,
        )[0:cs, :]
        * scale
    )
    stores[2].start()
    gwc_v[...] = (
        lax.dot_general(
            cot_all,
            fa[:, :, lo:].reshape(tokens, fa.shape[2] - lo),
            over_rows,
            preferred_element_type=jnp.float32,
        )[:, 0:cn]
        * scale
    )
    stores[3].start()
    for store in stores:
        store.wait()


def gather_shards(
    feat_sig,
    feat_cnx,
    cotangent,
    w_sig,
    w_cnx,
    lengths,
    enc_of,
    owner_of,
    pre_sig,
    pre_cnx,
    gain_sig,
    gain_cnx,
):
    n_enc, n_dp, n_rep = (lax.axis_size(axis) for axis in ("enc", "dp", "rep"))
    slots = lengths.shape[1]
    rows, chunk = cotangent.shape
    depth = rows // slots
    cs, cn = feat_sig.shape[1], feat_cnx.shape[1]
    whole = w_sig.shape[0]
    owners = n_dp * n_rep
    block = whole // owners
    joint = round_up(cs) + round_up(cn)
    bf16, f32 = jnp.bfloat16, jnp.float32
    dma = pltpu.SemaphoreType.DMA
    scratch = [
        pltpu.SMEM((1, slots), jnp.int32),
        pltpu.SMEM((1, slots), jnp.int32),
        pltpu.SMEM((1, slots), jnp.int32),
        pltpu.VMEM((rows, chunk), bf16),
        pltpu.VMEM((rows, cs), bf16),
        pltpu.VMEM((rows, cn), bf16),
        pltpu.VMEM((rows, cs), bf16),
        pltpu.VMEM((rows, cn), bf16),
        pltpu.VMEM((cs,), f32),
        pltpu.VMEM((cn,), f32),
        pltpu.VMEM((cs, whole), bf16),
        pltpu.VMEM((whole, cn), bf16),
        pltpu.VMEM((n_enc, rows, chunk), bf16),
        pltpu.VMEM((n_dp, depth, joint), bf16),
        pltpu.VMEM((n_dp, depth, joint), bf16),
        pltpu.VMEM((n_enc, rows, LANES), f32),
        pltpu.VMEM((n_enc, rows, LANES), f32),
        pltpu.VMEM((rows, joint), f32),
        pltpu.VMEM((rows, joint), f32),
        pltpu.VMEM((rows, joint), f32),
        dma((10,)),
        dma((2 * n_enc,)),
        dma((n_enc,)),
        dma((n_enc,)),
        dma((n_dp,)),
        dma((owners,)),
        dma((n_dp,)),
        dma((owners,)),
        dma((owners,)),
        dma((n_dp,)),
        dma((n_dp,)),
        dma((n_enc,)),
        dma((n_enc,)),
        dma((n_enc,)),
        dma((n_enc,)),
    ]
    hbm = pl.BlockSpec(memory_space=pltpu.HBM)
    vmem = pl.BlockSpec(memory_space=pltpu.VMEM)
    parts = pl.pallas_call(
        functools.partial(fused_kernel, (n_enc, n_dp, n_rep, slots, depth)),
        out_shape=(
            pltpu.VMEM((owners, rows, joint), bf16),
            pltpu.VMEM((owners, rows, block), bf16),
            pltpu.VMEM((rows, cs), bf16),
            pltpu.VMEM((rows, cn), bf16),
        ),
        in_specs=[hbm] * 12,
        out_specs=(vmem,) * 4,
        scratch_shapes=scratch,
        compiler_params=pltpu.CompilerParams(
            collective_id=0, has_side_effects=True, vmem_limit_bytes=VMEM_BYTES
        ),
        cost_estimate=pl.CostEstimate(
            flops=2 * rows * whole * (cs + cn),
            bytes_accessed=2 * whole * (cs + cn),
            transcendentals=2 * rows,
        ),
    )(
        lengths,
        enc_of,
        owner_of,
        cotangent,
        feat_sig,
        feat_cnx,
        pre_sig,
        pre_cnx,
        gain_sig,
        gain_cnx,
        w_sig.T,
        w_cnx,
    )
    grad_w_sig, *rest = pl.pallas_call(
        functools.partial(weight_kernel, 1.0 / math.sqrt(owners * rows)),
        out_shape=(
            jax.ShapeDtypeStruct((cs, block), f32),
            jax.ShapeDtypeStruct((block, cn), f32),
            jax.ShapeDtypeStruct((rows, cs), bf16),
            jax.ShapeDtypeStruct((rows, cn), bf16),
        ),
        in_specs=[vmem] * 4,
        out_specs=(hbm,) * 4,
        scratch_shapes=[pltpu.VMEM((cs, block), f32), pltpu.VMEM((block, cn), f32), dma((4,))],
        compiler_params=pltpu.CompilerParams(vmem_limit_bytes=VMEM_BYTES // 4),
        cost_estimate=pl.CostEstimate(
            flops=2 * rows * owners * block * (cs + cn),
            bytes_accessed=4 * block * (cs + cn),
            transcendentals=0,
        ),
    )(*parts)
    return (grad_w_sig.T, *rest)


def shards(feat_sig, feat_cnx, cotangent, w_sig, *others):
    n_enc, n_dp, n_rep = (lax.axis_size(axis) for axis in ("enc", "dp", "rep"))
    rows, chunk = cotangent.shape
    owners = n_dp * n_rep
    whole = w_sig.shape[0]
    gathered = owners * rows * (feat_sig.shape[1] + feat_cnx.shape[1]) * 2
    fits = gathered <= GATHER_BYTES and n_rep == 2 and rows % 16 == 0
    fits = fits and others[1].shape[1] == n_dp and whole % (owners * LANES) == 0
    fits = fits and chunk % (whole // owners) == 0
    form = gather_shards if fits else partial_sum_shards
    return form(feat_sig, feat_cnx, cotangent, w_sig, *others)


def solution(mesh):
    in_specs = (
        P(("dp", "rep"), "enc"),
        P(("dp", "rep"), "enc"),
        P(("dp", "rep"), "enc"),
        P(None, "enc"),
        P(None, "enc"),
        P(("dp", "rep"), None),
        P(("dp", "rep"), None),
        P(("dp", "rep"), None),
        P(("dp", "rep"), "enc"),
        P(("dp", "rep"), "enc"),
        P("enc"),
        P("enc"),
    )
    out_specs = (
        P(("dp", "rep"), "enc"),
        P(("dp", "rep"), "enc"),
        P(("dp", "rep"), "enc"),
        P(("dp", "rep"), "enc"),
    )
    return jax.shard_map(shards, mesh=mesh, in_specs=in_specs, out_specs=out_specs, check_vma=False)
```

```python
import functools
import math

import jax
import jax.numpy as jnp
from jax import lax
from jax.experimental import pallas as pl
from jax.experimental.pallas import tpu as pltpu
from jax.sharding import PartitionSpec as P

EPS = 1e-06
LANES = 128
GATHER_BYTES = 4 * 1024 * 1024
VMEM_BYTES = 58 * 1024 * 1024
MESH = pl.DeviceIdType.MESH


def row_statistics_pair(row_height, sum_h, sum_hh, feature_width):
    hidden_mean = sum_h[:, None] / feature_width
    var_h = sum_hh[:, None] / feature_width - hidden_mean * hidden_mean
    inverse_deviation = lax.rsqrt(var_h + EPS)
    return (hidden_mean, inverse_deviation, (row_height - hidden_mean) * inverse_deviation)


def partial_sum_shards(
    feat_sig,
    feat_cnx,
    cotangent,
    w_sig,
    w_cnx,
    lengths,
    enc_of,
    owner_of,
    pre_sig,
    pre_cnx,
    gain_sig,
    gain_cnx,
):
    slots = lengths.shape[1]
    rows = cotangent.shape[0]
    depth = rows // slots
    spots = lax.broadcasted_iota(jnp.int32, (slots, depth), 1)
    live = (spots < lengths[0][:, None]).reshape(rows, 1)
    masked = jnp.where(live, cotangent, jnp.zeros_like(cotangent))
    full_grad = lax.all_gather(masked, "enc", axis=1, tiled=True)
    back_sig = jnp.dot(full_grad, w_sig, preferred_element_type=jnp.float32).astype(jnp.bfloat16)
    back_cnx = jnp.dot(full_grad, w_cnx, preferred_element_type=jnp.float32).astype(jnp.bfloat16)
    inverse = jnp.argsort(enc_of[0])
    send_sig = jnp.take(back_sig.reshape(slots, depth, back_sig.shape[1]), inverse, axis=0)
    send_cnx = jnp.take(back_cnx.reshape(slots, depth, back_cnx.shape[1]), inverse, axis=0)
    recv_sig, recv_cnx = (
        lax.all_to_all(send_sig, "dp", split_axis=0, concat_axis=0, tiled=True),
        lax.all_to_all(send_cnx, "dp", split_axis=0, concat_axis=0, tiled=True),
    )
    sources = owner_of[0]
    dy_sig = jnp.take(recv_sig, sources, axis=0).reshape(rows, recv_sig.shape[2])
    dy_cnx = jnp.take(recv_cnx, sources, axis=0).reshape(rows, recv_cnx.shape[2])
    enc_count = lax.axis_size("enc")
    siglip_width = gain_sig.shape[0] * enc_count
    convnext_width = gain_cnx.shape[0] * enc_count
    siglip_height = pre_sig.astype(jnp.float32)
    convnext_height = pre_cnx.astype(jnp.float32)
    siglip_scaled_gradient = dy_sig.astype(jnp.float32) * gain_sig
    convnext_scaled_gradient = dy_cnx.astype(jnp.float32) * gain_cnx
    row_totals = lax.psum(
        (
            jnp.sum(siglip_height, axis=1),
            jnp.sum(siglip_height * siglip_height, axis=1),
            jnp.sum(convnext_height, axis=1),
            jnp.sum(convnext_height * convnext_height, axis=1),
        ),
        "enc",
    )
    siglip_mean, siglip_inverse_deviation, siglip_normalized = row_statistics_pair(
        siglip_height, row_totals[0], row_totals[1], siglip_width
    )
    convnext_mean, convnext_inverse_deviation, convnext_normalized = row_statistics_pair(
        convnext_height, row_totals[2], row_totals[3], convnext_width
    )
    later = lax.psum(
        (
            jnp.sum(siglip_scaled_gradient, axis=1),
            jnp.sum(siglip_scaled_gradient * siglip_normalized, axis=1),
            jnp.sum(convnext_scaled_gradient, axis=1),
            jnp.sum(convnext_scaled_gradient * convnext_normalized, axis=1),
        ),
        "enc",
    )
    siglip_gradient_mean = later[0][:, None] / siglip_width
    siglip_product_mean = later[1][:, None] / siglip_width
    convnext_gradient_mean = later[2][:, None] / convnext_width
    convnext_product_mean = later[3][:, None] / convnext_width
    gradient_before_siglip = (
        siglip_inverse_deviation
        * (siglip_scaled_gradient - siglip_gradient_mean - siglip_normalized * siglip_product_mean)
    ).astype(jnp.bfloat16)
    gradient_before_convnext = (
        convnext_inverse_deviation
        * (
            convnext_scaled_gradient
            - convnext_gradient_mean
            - convnext_normalized * convnext_product_mean
        )
    ).astype(jnp.bfloat16)
    dp_count = lax.axis_size("dp")
    rep_count = lax.axis_size("rep")
    scale = 1.0 / math.sqrt(rows * dp_count * rep_count)
    split = feat_sig.shape[1]
    features = jnp.concatenate([feat_sig, feat_cnx], axis=1)
    summed = lax.psum_scatter(
        lax.dot_general(
            full_grad, features, (((0,), (0,)), ((), ())), preferred_element_type=jnp.float32
        ),
        ("dp", "rep"),
        scatter_dimension=0,
        tiled=True,
    )
    summed = summed * scale
    return (summed[:, :split], summed[:, split:], gradient_before_siglip, gradient_before_convnext)


def round_up(width):
    return -(-width // LANES) * LANES


def fused_kernel(
    sizes,
    lengths_hbm,
    enc_of_hbm,
    owner_of_hbm,
    cot_hbm,
    fs_hbm,
    fc_hbm,
    ps_hbm,
    pc_hbm,
    gs_hbm,
    gc_hbm,
    ws_hbm,
    wc_hbm,
    fa,
    cc,
    os_ref,
    oc_ref,
    len_s,
    enc_s,
    own_s,
    cot_v,
    fs_v,
    fc_v,
    ps_v,
    pc_v,
    gs_v,
    gc_v,
    ws_v,
    wc_v,
    fg,
    sb,
    rb,
    st1,
    st2,
    joint,
    height,
    dy,
    local_sem,
    w_sem,
    fg_send,
    fg_recv,
    fa_send,
    fa_recv,
    relay_send,
    fwd_send,
    cc_send,
    cc_recv,
    rb_send,
    rb_recv,
    st1_send,
    st1_recv,
    st2_send,
    st2_recv,
):
    n_enc, n_dp, n_rep, slots, depth = sizes
    rows = slots * depth
    e, d, r = lax.axis_index("enc"), lax.axis_index("dp"), lax.axis_index("rep")
    chunk = cot_v.shape[1]
    cs, cn = fs_v.shape[1], fc_v.shape[1]
    lo = round_up(cs)
    block = cc.shape[2]
    per = chunk // block
    width_s, width_c = cs * n_enc, cn * n_enc
    b = d * n_rep + r
    enc_peers = [lax.rem(e + k, n_enc) for k in range(1, n_enc)]
    dp_peers = [lax.rem(d + k, n_dp) for k in range(1, n_dp)]
    partner = 1 - r
    half = n_dp // 2
    side = d // half
    mates = [side * half + lax.rem(d + k, half) for k in range(1, half)]
    crossed = [(1 - side) * half + k for k in range(half)]
    gateway = half - 1 + side
    far_gateway = half - side
    is_gateway = d == gateway

    barrier = pltpu.get_barrier_semaphore()
    for p in enc_peers:
        pl.semaphore_signal(barrier, inc=1, device_id=(p, d, r), device_id_type=MESH)
    for q in dp_peers:
        for s in range(n_rep):
            pl.semaphore_signal(barrier, inc=1, device_id=(e, q, s), device_id_type=MESH)
    pl.semaphore_signal(barrier, inc=1, device_id=(e, d, partner), device_id_type=MESH)

    pairs = (
        (lengths_hbm, len_s),
        (enc_of_hbm, enc_s),
        (owner_of_hbm, own_s),
        (cot_hbm, cot_v),
        (fs_hbm, fs_v),
        (fc_hbm, fc_v),
        (ps_hbm, ps_v),
        (pc_hbm, pc_v),
        (gs_hbm, gs_v),
        (gc_hbm, gc_v),
    )
    loads = [
        pltpu.make_async_copy(source, target, local_sem.at[i])
        for i, (source, target) in enumerate(pairs)
    ]
    for load in loads:
        load.start()
    w_loads = []
    for k in range(n_enc):
        p = lax.rem(e + k, n_enc)
        at = pl.ds(pl.multiple_of(p * chunk, chunk), chunk)
        pair = (
            pltpu.make_async_copy(ws_hbm.at[:, at], ws_v.at[:, at], w_sem.at[2 * k]),
            pltpu.make_async_copy(wc_hbm.at[at], wc_v.at[at], w_sem.at[2 * k + 1]),
        )
        for load in pair:
            load.start()
        w_loads.append(pair)

    for i in range(4):
        loads[i].wait()
    row = lax.broadcasted_iota(jnp.int32, (rows, rows), 0)
    col = lax.broadcasted_iota(jnp.int32, (rows, rows), 1)
    same_spot = lax.rem(row, depth) == lax.rem(col, depth)
    pick = jnp.zeros((rows, rows), jnp.float32)
    for j in range(slots):
        taken = (col // depth == j) & (row // depth == enc_s[0, j])
        taken = taken & same_spot & (lax.rem(col, depth) < len_s[0, j])
        pick = jnp.where(taken, 1.0, pick)
    pick = pick.astype(jnp.bfloat16)
    mine = jnp.dot(pick, cot_v[...], preferred_element_type=jnp.float32).astype(jnp.bfloat16)
    fg[e] = mine

    pl.semaphore_wait(barrier, n_enc - 1 + n_dp * n_rep - 1)

    sent = []

    def send(src, dst, send_sem, recv_sem, device):
        copy = pltpu.make_async_remote_copy(
            src_ref=src,
            dst_ref=dst,
            send_sem=send_sem,
            recv_sem=recv_sem,
            device_id=device,
            device_id_type=MESH,
        )
        copy.start()
        sent.append(copy)

    def arrived(dst, recv_sem, device):
        pltpu.make_async_remote_copy(
            src_ref=dst,
            dst_ref=dst,
            send_sem=recv_sem,
            recv_sem=recv_sem,
            device_id=device,
            device_id_type=MESH,
        ).wait_recv()

    for k, p in enumerate(enc_peers):
        send(fg.at[e], fg.at[e], fg_send.at[k], fg_recv.at[e], (p, d, r))

    loads[4].wait()
    loads[5].wait()
    fa[b] = jnp.zeros_like(fa[b])
    fa[b, :, 0:cs] = jnp.dot(pick, fs_v[...], preferred_element_type=jnp.float32).astype(
        jnp.bfloat16
    )
    fa[b, :, lo : lo + cn] = jnp.dot(
        pick, fc_v[...], preferred_element_type=jnp.float32
    ).astype(jnp.bfloat16)
    send(fa.at[b], fa.at[b], fa_send.at[0], fa_recv.at[b], (e, far_gateway, r))
    send(fa.at[b], fa.at[b], fa_send.at[1], fa_recv.at[b], (e, d, partner))
    for k, q in enumerate(mates):
        send(fa.at[b], fa.at[b], fa_send.at[2 + k], fa_recv.at[b], (e, q, r))

    loads[6].wait()
    loads[7].wait()
    height[...] = jnp.zeros_like(height)
    height[:, 0:cs] = ps_v[...].astype(jnp.float32)
    height[:, lo : lo + cn] = pc_v[...].astype(jnp.float32)
    h_s, h_c = height[:, 0:lo], height[:, lo:]
    lane = lax.broadcasted_iota(jnp.int32, (rows, LANES), 1)

    def four(values):
        sums = [jnp.sum(v, axis=1, keepdims=True) for v in values]
        packed = jnp.zeros((rows, LANES), jnp.float32)
        for i, total in enumerate(sums):
            packed = jnp.where(lane == i, total, packed)
        return packed

    st1[e] = four((h_s, h_s * h_s, h_c, h_c * h_c))
    for k, p in enumerate(enc_peers):
        send(st1.at[e], st1.at[e], st1_send.at[k], st1_recv.at[e], (p, d, r))

    acc_s = jnp.zeros((rows, cs), jnp.float32)
    acc_c = jnp.zeros((rows, cn), jnp.float32)
    for k in range(n_enc):
        p = lax.rem(e + k, n_enc)
        at = pl.ds(pl.multiple_of(p * chunk, chunk), chunk)
        for load in w_loads[k]:
            load.wait()
        if k > 0:
            arrived(fg.at[p], fg_recv.at[p], (p, d, r))
        part = fg[p]
        acc_s += lax.dot_general(
            part, ws_v[:, at], (((1,), (1,)), ((), ())), preferred_element_type=jnp.float32
        )
        acc_c += jnp.dot(part, wc_v[at, :], preferred_element_type=jnp.float32)
    joint[...] = jnp.zeros_like(joint)
    joint[:, 0:cs] = acc_s
    joint[:, lo : lo + cn] = acc_c
    for i in range(slots):
        sb[i] = joint[i * depth : (i + 1) * depth, :].astype(jnp.bfloat16)
    rb[d] = sb[d]
    for k, q in enumerate(dp_peers):
        send(sb.at[q], rb.at[d], rb_send.at[k], rb_recv.at[d], (e, q, r))

    def relay():
        copies = []
        for k, q in enumerate(crossed):
            at = q * n_rep + r
            for m, mate in enumerate(mates):
                copies.append(
                    pltpu.make_async_remote_copy(
                        src_ref=fa.at[at],
                        dst_ref=fa.at[at],
                        send_sem=relay_send.at[k * (half - 1) + m],
                        recv_sem=fa_recv.at[at],
                        device_id=(e, mate, r),
                        device_id_type=MESH,
                    )
                )
        return copies

    @pl.when(is_gateway)
    def _():
        for q in crossed:
            arrived(fa.at[q * n_rep + r], fa_recv.at[q * n_rep + r], (e, q, r))
        for copy in relay():
            copy.start()

    for p in enc_peers:
        arrived(st1.at[p], st1_recv.at[p], (p, d, r))
    total = st1[0]
    for i in range(1, n_enc):
        total += st1[i]

    def normalize(h, sum_h, sum_hh, width):
        mean = sum_h / width
        rstd = lax.rsqrt(sum_hh / width - mean * mean + EPS)
        return rstd, (h - mean) * rstd

    rstd_s, xhat_s = normalize(h_s, total[:, 0:1], total[:, 1:2], width_s)
    rstd_c, xhat_c = normalize(h_c, total[:, 2:3], total[:, 3:4], width_c)

    for k, q in enumerate(mates):
        at = q * n_rep + r
        arrived(fa.at[at], fa_recv.at[at], (e, q, r))
        send(fa.at[at], fa.at[at], fwd_send.at[half + k], fa_recv.at[at], (e, d, partner))

    for q in dp_peers:
        arrived(rb.at[q], rb_recv.at[q], (e, q, r))
    pieces = [rb[o].astype(jnp.float32) for o in range(n_dp)]
    for i in range(slots):
        chosen = pieces[0]
        for o in range(1, n_dp):
            chosen = jnp.where(own_s[0, i] == o, pieces[o], chosen)
        dy[i * depth : (i + 1) * depth, :] = chosen
    loads[8].wait()
    loads[9].wait()
    joint[...] = jnp.zeros_like(joint)
    joint[:, 0:cs] = dy[:, 0:cs] * gs_v[...].reshape(1, cs)
    joint[:, lo : lo + cn] = dy[:, lo : lo + cn] * gc_v[...].reshape(1, cn)
    gy_s, gy_c = joint[:, 0:lo], joint[:, lo:]
    st2[e] = four((gy_s, gy_s * xhat_s, gy_c, gy_c * xhat_c))
    for k, p in enumerate(enc_peers):
        send(st2.at[e], st2.at[e], st2_send.at[k], st2_recv.at[e], (p, d, r))

    def my_block(q, s):
        first = q * n_rep + s
        return fg.at[first // per, :, pl.ds(pl.multiple_of(lax.rem(first, per) * block, block), block)]

    cc[b] = my_block(d, r)[...]
    count = 0
    for q in dp_peers:
        for s in range(n_rep):
            send(my_block(q, s), cc.at[b], cc_send.at[count], cc_recv.at[b], (e, q, s))
            count += 1
    send(my_block(d, partner), cc.at[b], cc_send.at[count], cc_recv.at[b], (e, d, partner))

    @pl.when(jnp.logical_not(is_gateway))
    def _():
        for q in crossed:
            arrived(fa.at[q * n_rep + r], fa_recv.at[q * n_rep + r], (e, gateway, r))

    for k, q in enumerate(crossed):
        at = q * n_rep + r
        send(fa.at[at], fa.at[at], fwd_send.at[k], fa_recv.at[at], (e, d, partner))

    for p in enc_peers:
        arrived(st2.at[p], st2_recv.at[p], (p, d, r))
    later = st2[0]
    for i in range(1, n_enc):
        later += st2[i]
    mean_s, prod_s = later[:, 0:1] / width_s, later[:, 1:2] / width_s
    mean_c, prod_c = later[:, 2:3] / width_c, later[:, 3:4] / width_c
    os_ref[...] = (rstd_s * (gy_s - mean_s - xhat_s * prod_s))[:, 0:cs].astype(os_ref.dtype)
    oc_ref[...] = (rstd_c * (gy_c - mean_c - xhat_c * prod_c))[:, 0:cn].astype(oc_ref.dtype)

    for q in dp_peers:
        for s in range(n_rep):
            at = q * n_rep + s
            arrived(cc.at[at], cc_recv.at[at], (e, q, s))
        other = q * n_rep + partner
        arrived(fa.at[other], fa_recv.at[other], (e, d, partner))
    beside = d * n_rep + partner
    arrived(cc.at[beside], cc_recv.at[beside], (e, d, partner))
    arrived(fa.at[beside], fa_recv.at[beside], (e, d, partner))

    for copy in sent:
        copy.wait_send()

    @pl.when(is_gateway)
    def _():
        for copy in relay():
            copy.wait_send()


def weight_kernel(
    scale, fa, cc, os_v, oc_v, gws_hbm, gwc_hbm, os_hbm, oc_hbm, gws_v, gwc_v, out_sem
):
    tokens = cc.shape[0] * cc.shape[1]
    cs, cn = gws_v.shape[0], gwc_v.shape[1]
    lo = round_up(cs)
    stores = [
        pltpu.make_async_copy(os_v, os_hbm, out_sem.at[0]),
        pltpu.make_async_copy(oc_v, oc_hbm, out_sem.at[1]),
        pltpu.make_async_copy(gws_v, gws_hbm, out_sem.at[2]),
        pltpu.make_async_copy(gwc_v, gwc_hbm, out_sem.at[3]),
    ]
    stores[0].start()
    stores[1].start()
    cot_all = cc[...].reshape(tokens, cc.shape[2])
    over_rows = (((0,), (0,)), ((), ()))
    gws_v[...] = (
        lax.dot_general(
            fa[:, :, 0:lo].reshape(tokens, lo),
            cot_all,
            over_rows,
            preferred_element_type=jnp.float32,
        )[0:cs, :]
        * scale
    )
    stores[2].start()
    gwc_v[...] = (
        lax.dot_general(
            cot_all,
            fa[:, :, lo:].reshape(tokens, fa.shape[2] - lo),
            over_rows,
            preferred_element_type=jnp.float32,
        )[:, 0:cn]
        * scale
    )
    stores[3].start()
    for store in stores:
        store.wait()


def gather_shards(
    feat_sig,
    feat_cnx,
    cotangent,
    w_sig,
    w_cnx,
    lengths,
    enc_of,
    owner_of,
    pre_sig,
    pre_cnx,
    gain_sig,
    gain_cnx,
):
    n_enc, n_dp, n_rep = (lax.axis_size(axis) for axis in ("enc", "dp", "rep"))
    slots = lengths.shape[1]
    rows, chunk = cotangent.shape
    depth = rows // slots
    cs, cn = feat_sig.shape[1], feat_cnx.shape[1]
    whole = w_sig.shape[0]
    owners = n_dp * n_rep
    block = whole // owners
    joint = round_up(cs) + round_up(cn)
    bf16, f32 = jnp.bfloat16, jnp.float32
    dma = pltpu.SemaphoreType.DMA
    scratch = [
        pltpu.SMEM((1, slots), jnp.int32),
        pltpu.SMEM((1, slots), jnp.int32),
        pltpu.SMEM((1, slots), jnp.int32),
        pltpu.VMEM((rows, chunk), bf16),
        pltpu.VMEM((rows, cs), bf16),
        pltpu.VMEM((rows, cn), bf16),
        pltpu.VMEM((rows, cs), bf16),
        pltpu.VMEM((rows, cn), bf16),
        pltpu.VMEM((cs,), f32),
        pltpu.VMEM((cn,), f32),
        pltpu.VMEM((cs, whole), bf16),
        pltpu.VMEM((whole, cn), bf16),
        pltpu.VMEM((n_enc, rows, chunk), bf16),
        pltpu.VMEM((n_dp, depth, joint), bf16),
        pltpu.VMEM((n_dp, depth, joint), bf16),
        pltpu.VMEM((n_enc, rows, LANES), f32),
        pltpu.VMEM((n_enc, rows, LANES), f32),
        pltpu.VMEM((rows, joint), f32),
        pltpu.VMEM((rows, joint), f32),
        pltpu.VMEM((rows, joint), f32),
        dma((10,)),
        dma((2 * n_enc,)),
        dma((n_enc,)),
        dma((n_enc,)),
        dma((n_dp,)),
        dma((owners,)),
        dma((n_dp * n_dp,)),
        dma((n_dp,)),
        dma((owners,)),
        dma((owners,)),
        dma((n_dp,)),
        dma((n_dp,)),
        dma((n_enc,)),
        dma((n_enc,)),
        dma((n_enc,)),
        dma((n_enc,)),
    ]
    hbm = pl.BlockSpec(memory_space=pltpu.HBM)
    vmem = pl.BlockSpec(memory_space=pltpu.VMEM)
    parts = pl.pallas_call(
        functools.partial(fused_kernel, (n_enc, n_dp, n_rep, slots, depth)),
        out_shape=(
            pltpu.VMEM((owners, rows, joint), bf16),
            pltpu.VMEM((owners, rows, block), bf16),
            pltpu.VMEM((rows, cs), bf16),
            pltpu.VMEM((rows, cn), bf16),
        ),
        in_specs=[hbm] * 12,
        out_specs=(vmem,) * 4,
        scratch_shapes=scratch,
        compiler_params=pltpu.CompilerParams(
            collective_id=0, has_side_effects=True, vmem_limit_bytes=VMEM_BYTES
        ),
        cost_estimate=pl.CostEstimate(
            flops=2 * rows * whole * (cs + cn),
            bytes_accessed=2 * whole * (cs + cn),
            transcendentals=2 * rows,
        ),
    )(
        lengths,
        enc_of,
        owner_of,
        cotangent,
        feat_sig,
        feat_cnx,
        pre_sig,
        pre_cnx,
        gain_sig,
        gain_cnx,
        w_sig.T,
        w_cnx,
    )
    grad_w_sig, *rest = pl.pallas_call(
        functools.partial(weight_kernel, 1.0 / math.sqrt(owners * rows)),
        out_shape=(
            jax.ShapeDtypeStruct((cs, block), f32),
            jax.ShapeDtypeStruct((block, cn), f32),
            jax.ShapeDtypeStruct((rows, cs), bf16),
            jax.ShapeDtypeStruct((rows, cn), bf16),
        ),
        in_specs=[vmem] * 4,
        out_specs=(hbm,) * 4,
        scratch_shapes=[pltpu.VMEM((cs, block), f32), pltpu.VMEM((block, cn), f32), dma((4,))],
        compiler_params=pltpu.CompilerParams(vmem_limit_bytes=VMEM_BYTES // 4),
        cost_estimate=pl.CostEstimate(
            flops=2 * rows * owners * block * (cs + cn),
            bytes_accessed=4 * block * (cs + cn),
            transcendentals=0,
        ),
    )(*parts)
    return (grad_w_sig.T, *rest)


def shards(feat_sig, feat_cnx, cotangent, w_sig, *others):
    n_enc, n_dp, n_rep = (lax.axis_size(axis) for axis in ("enc", "dp", "rep"))
    rows, chunk = cotangent.shape
    owners = n_dp * n_rep
    whole = w_sig.shape[0]
    gathered = owners * rows * (feat_sig.shape[1] + feat_cnx.shape[1]) * 2
    fits = gathered <= GATHER_BYTES and n_rep == 2 and n_dp % 2 == 0 and rows % 16 == 0
    fits = fits and others[1].shape[1] == n_dp and whole % (owners * LANES) == 0
    fits = fits and chunk % (whole // owners) == 0
    form = gather_shards if fits else partial_sum_shards
    return form(feat_sig, feat_cnx, cotangent, w_sig, *others)


def solution(mesh):
    in_specs = (
        P(("dp", "rep"), "enc"),
        P(("dp", "rep"), "enc"),
        P(("dp", "rep"), "enc"),
        P(None, "enc"),
        P(None, "enc"),
        P(("dp", "rep"), None),
        P(("dp", "rep"), None),
        P(("dp", "rep"), None),
        P(("dp", "rep"), "enc"),
        P(("dp", "rep"), "enc"),
        P("enc"),
        P("enc"),
    )
    out_specs = (
        P(("dp", "rep"), "enc"),
        P(("dp", "rep"), "enc"),
        P(("dp", "rep"), "enc"),
        P(("dp", "rep"), "enc"),
    )
    return jax.shard_map(shards, mesh=mesh, in_specs=in_specs, out_specs=out_specs, check_vma=False)
```

```python
import functools
import math

import jax
import jax.numpy as jnp
from jax import lax
from jax.experimental import pallas as pl
from jax.experimental.pallas import tpu as pltpu
from jax.sharding import PartitionSpec as P

EPS = 1e-06
LANES = 128
GATHER_BYTES = 4 * 1024 * 1024
VMEM_BYTES = 58 * 1024 * 1024
MESH = pl.DeviceIdType.MESH


def row_statistics_pair(row_height, sum_h, sum_hh, feature_width):
    hidden_mean = sum_h[:, None] / feature_width
    var_h = sum_hh[:, None] / feature_width - hidden_mean * hidden_mean
    inverse_deviation = lax.rsqrt(var_h + EPS)
    return (hidden_mean, inverse_deviation, (row_height - hidden_mean) * inverse_deviation)


def partial_sum_shards(
    feat_sig,
    feat_cnx,
    cotangent,
    w_sig,
    w_cnx,
    lengths,
    enc_of,
    owner_of,
    pre_sig,
    pre_cnx,
    gain_sig,
    gain_cnx,
):
    slots = lengths.shape[1]
    rows = cotangent.shape[0]
    depth = rows // slots
    spots = lax.broadcasted_iota(jnp.int32, (slots, depth), 1)
    live = (spots < lengths[0][:, None]).reshape(rows, 1)
    masked = jnp.where(live, cotangent, jnp.zeros_like(cotangent))
    full_grad = lax.all_gather(masked, "enc", axis=1, tiled=True)
    back_sig = jnp.dot(full_grad, w_sig, preferred_element_type=jnp.float32).astype(jnp.bfloat16)
    back_cnx = jnp.dot(full_grad, w_cnx, preferred_element_type=jnp.float32).astype(jnp.bfloat16)
    inverse = jnp.argsort(enc_of[0])
    send_sig = jnp.take(back_sig.reshape(slots, depth, back_sig.shape[1]), inverse, axis=0)
    send_cnx = jnp.take(back_cnx.reshape(slots, depth, back_cnx.shape[1]), inverse, axis=0)
    recv_sig, recv_cnx = (
        lax.all_to_all(send_sig, "dp", split_axis=0, concat_axis=0, tiled=True),
        lax.all_to_all(send_cnx, "dp", split_axis=0, concat_axis=0, tiled=True),
    )
    sources = owner_of[0]
    dy_sig = jnp.take(recv_sig, sources, axis=0).reshape(rows, recv_sig.shape[2])
    dy_cnx = jnp.take(recv_cnx, sources, axis=0).reshape(rows, recv_cnx.shape[2])
    enc_count = lax.axis_size("enc")
    siglip_width = gain_sig.shape[0] * enc_count
    convnext_width = gain_cnx.shape[0] * enc_count
    siglip_height = pre_sig.astype(jnp.float32)
    convnext_height = pre_cnx.astype(jnp.float32)
    siglip_scaled_gradient = dy_sig.astype(jnp.float32) * gain_sig
    convnext_scaled_gradient = dy_cnx.astype(jnp.float32) * gain_cnx
    row_totals = lax.psum(
        (
            jnp.sum(siglip_height, axis=1),
            jnp.sum(siglip_height * siglip_height, axis=1),
            jnp.sum(convnext_height, axis=1),
            jnp.sum(convnext_height * convnext_height, axis=1),
        ),
        "enc",
    )
    siglip_mean, siglip_inverse_deviation, siglip_normalized = row_statistics_pair(
        siglip_height, row_totals[0], row_totals[1], siglip_width
    )
    convnext_mean, convnext_inverse_deviation, convnext_normalized = row_statistics_pair(
        convnext_height, row_totals[2], row_totals[3], convnext_width
    )
    later = lax.psum(
        (
            jnp.sum(siglip_scaled_gradient, axis=1),
            jnp.sum(siglip_scaled_gradient * siglip_normalized, axis=1),
            jnp.sum(convnext_scaled_gradient, axis=1),
            jnp.sum(convnext_scaled_gradient * convnext_normalized, axis=1),
        ),
        "enc",
    )
    siglip_gradient_mean = later[0][:, None] / siglip_width
    siglip_product_mean = later[1][:, None] / siglip_width
    convnext_gradient_mean = later[2][:, None] / convnext_width
    convnext_product_mean = later[3][:, None] / convnext_width
    gradient_before_siglip = (
        siglip_inverse_deviation
        * (siglip_scaled_gradient - siglip_gradient_mean - siglip_normalized * siglip_product_mean)
    ).astype(jnp.bfloat16)
    gradient_before_convnext = (
        convnext_inverse_deviation
        * (
            convnext_scaled_gradient
            - convnext_gradient_mean
            - convnext_normalized * convnext_product_mean
        )
    ).astype(jnp.bfloat16)
    dp_count = lax.axis_size("dp")
    rep_count = lax.axis_size("rep")
    scale = 1.0 / math.sqrt(rows * dp_count * rep_count)
    split = feat_sig.shape[1]
    features = jnp.concatenate([feat_sig, feat_cnx], axis=1)
    summed = lax.psum_scatter(
        lax.dot_general(
            full_grad, features, (((0,), (0,)), ((), ())), preferred_element_type=jnp.float32
        ),
        ("dp", "rep"),
        scatter_dimension=0,
        tiled=True,
    )
    summed = summed * scale
    return (summed[:, :split], summed[:, split:], gradient_before_siglip, gradient_before_convnext)


def round_up(width):
    return -(-width // LANES) * LANES


def fused_kernel(
    sizes,
    lengths_hbm,
    enc_of_hbm,
    owner_of_hbm,
    cot_hbm,
    fs_hbm,
    fc_hbm,
    ps_hbm,
    pc_hbm,
    gs_hbm,
    gc_hbm,
    ws_hbm,
    wc_hbm,
    fa,
    cc,
    os_ref,
    oc_ref,
    len_s,
    enc_s,
    own_s,
    fs_v,
    fc_v,
    ps_v,
    pc_v,
    gs_v,
    gc_v,
    ws_v,
    wc_v,
    fg,
    sb,
    rb,
    st1,
    st2,
    joint,
    height,
    dy,
    local_sem,
    w_sem,
    fg_send,
    fg_recv,
    fa_send,
    fa_recv,
    fwd_send,
    cc_send,
    cc_recv,
    rb_send,
    rb_recv,
    st1_send,
    st1_recv,
    st2_send,
    st2_recv,
):
    n_enc, n_dp, n_rep, slots, depth = sizes
    rows = slots * depth
    e, d, r = lax.axis_index("enc"), lax.axis_index("dp"), lax.axis_index("rep")
    chunk = cot_hbm.shape[1]
    cs, cn = fs_v.shape[1], fc_v.shape[1]
    lo = round_up(cs)
    block = cc.shape[2]
    per = chunk // block
    width_s, width_c = cs * n_enc, cn * n_enc
    b = d * n_rep + r
    enc_peers = [lax.rem(e + k, n_enc) for k in range(1, n_enc)]
    dp_peers = [lax.rem(d + k, n_dp) for k in range(1, n_dp)]
    partner = 1 - r

    barrier = pltpu.get_barrier_semaphore()
    for p in enc_peers:
        pl.semaphore_signal(barrier, inc=1, device_id=(p, d, r), device_id_type=MESH)
    for q in dp_peers:
        for s in range(n_rep):
            pl.semaphore_signal(barrier, inc=1, device_id=(e, q, s), device_id_type=MESH)
    pl.semaphore_signal(barrier, inc=1, device_id=(e, d, partner), device_id_type=MESH)

    pairs = (
        (lengths_hbm, len_s),
        (enc_of_hbm, enc_s),
        (owner_of_hbm, own_s),
        (cot_hbm, fg.at[e]),
        (fs_hbm, fs_v),
        (fc_hbm, fc_v),
        (ps_hbm, ps_v),
        (pc_hbm, pc_v),
        (gs_hbm, gs_v),
        (gc_hbm, gc_v),
    )
    loads = [
        pltpu.make_async_copy(source, target, local_sem.at[i])
        for i, (source, target) in enumerate(pairs)
    ]
    for load in loads:
        load.start()
    w_loads = []
    for k in range(n_enc):
        p = lax.rem(e + k, n_enc)
        at = pl.ds(pl.multiple_of(p * chunk, chunk), chunk)
        pair = (
            pltpu.make_async_copy(ws_hbm.at[:, at], ws_v.at[:, at], w_sem.at[2 * k]),
            pltpu.make_async_copy(wc_hbm.at[at], wc_v.at[at], w_sem.at[2 * k + 1]),
        )
        for load in pair:
            load.start()
        w_loads.append(pair)

    pl.semaphore_wait(barrier, n_enc - 1 + n_dp * n_rep - 1)

    sent = []

    def send(src, dst, send_sem, recv_sem, device):
        copy = pltpu.make_async_remote_copy(
            src_ref=src,
            dst_ref=dst,
            send_sem=send_sem,
            recv_sem=recv_sem,
            device_id=device,
            device_id_type=MESH,
        )
        copy.start()
        sent.append(copy)

    def arrived(dst, recv_sem, device):
        pltpu.make_async_remote_copy(
            src_ref=dst,
            dst_ref=dst,
            send_sem=recv_sem,
            recv_sem=recv_sem,
            device_id=device,
            device_id_type=MESH,
        ).wait_recv()

    for k, p in enumerate(enc_peers):
        send(cot_hbm, fg.at[e], fg_send.at[k], fg_recv.at[e], (p, d, r))

    for i in (0, 1, 2, 4, 5):
        loads[i].wait()
    row = lax.broadcasted_iota(jnp.int32, (rows, 1), 0)
    live = jnp.zeros((rows, 1), jnp.float32)
    for j in range(slots):
        spot = row - j * depth
        live = jnp.where((spot >= 0) & (spot < len_s[0, j]), 1.0, live)
    fa[b] = jnp.zeros_like(fa[b])
    fa[b, :, 0:cs] = (fs_v[...].astype(jnp.float32) * live).astype(jnp.bfloat16)
    fa[b, :, lo : lo + cn] = (fc_v[...].astype(jnp.float32) * live).astype(jnp.bfloat16)
    for k, q in enumerate(dp_peers):
        send(fa.at[b], fa.at[b], fa_send.at[k], fa_recv.at[b], (e, q, r))
    send(fa.at[b], fa.at[b], fa_send.at[n_dp - 1], fa_recv.at[b], (e, d, partner))

    loads[6].wait()
    loads[7].wait()
    height[...] = jnp.zeros_like(height)
    height[:, 0:cs] = ps_v[...].astype(jnp.float32)
    height[:, lo : lo + cn] = pc_v[...].astype(jnp.float32)
    h_s, h_c = height[:, 0:lo], height[:, lo:]
    lane = lax.broadcasted_iota(jnp.int32, (rows, LANES), 1)

    def four(values):
        sums = [jnp.sum(v, axis=1, keepdims=True) for v in values]
        packed = jnp.zeros((rows, LANES), jnp.float32)
        for i, total in enumerate(sums):
            packed = jnp.where(lane == i, total, packed)
        return packed

    st1[e] = four((h_s, h_s * h_s, h_c, h_c * h_c))
    for k, p in enumerate(enc_peers):
        send(st1.at[e], st1.at[e], st1_send.at[k], st1_recv.at[e], (p, d, r))

    acc_s = jnp.zeros((rows, cs), jnp.float32)
    acc_c = jnp.zeros((rows, cn), jnp.float32)
    for k in range(n_enc):
        p = lax.rem(e + k, n_enc)
        at = pl.ds(pl.multiple_of(p * chunk, chunk), chunk)
        for load in w_loads[k]:
            load.wait()
        if k == 0:
            loads[3].wait()
        else:
            arrived(fg.at[p], fg_recv.at[p], (p, d, r))
        part = fg[p]
        acc_s += lax.dot_general(
            part, ws_v[:, at], (((1,), (1,)), ((), ())), preferred_element_type=jnp.float32
        )
        acc_c += jnp.dot(part, wc_v[at, :], preferred_element_type=jnp.float32)
    joint[...] = jnp.zeros_like(joint)
    joint[:, 0:cs] = acc_s * live
    joint[:, lo : lo + cn] = acc_c * live
    slices = [joint[j * depth : (j + 1) * depth, :] for j in range(slots)]
    for i in range(n_dp):
        chosen = slices[0]
        for j in range(1, slots):
            chosen = jnp.where(enc_s[0, j] == i, slices[j], chosen)
        sb[i] = chosen.astype(jnp.bfloat16)
    rb[d] = sb[d]
    for k, q in enumerate(dp_peers):
        send(sb.at[q], rb.at[d], rb_send.at[k], rb_recv.at[d], (e, q, r))

    def my_block(q, s):
        first = q * n_rep + s
        return fg.at[first // per, :, pl.ds(pl.multiple_of(lax.rem(first, per) * block, block), block)]

    cc[b] = my_block(d, r)[...]
    count = 0
    for q in dp_peers:
        for s in range(n_rep):
            send(my_block(q, s), cc.at[b], cc_send.at[count], cc_recv.at[b], (e, q, s))
            count += 1
    send(my_block(d, partner), cc.at[b], cc_send.at[count], cc_recv.at[b], (e, d, partner))

    for p in enc_peers:
        arrived(st1.at[p], st1_recv.at[p], (p, d, r))
    total = st1[0]
    for i in range(1, n_enc):
        total += st1[i]

    def normalize(h, sum_h, sum_hh, width):
        mean = sum_h / width
        rstd = lax.rsqrt(sum_hh / width - mean * mean + EPS)
        return rstd, (h - mean) * rstd

    rstd_s, xhat_s = normalize(h_s, total[:, 0:1], total[:, 1:2], width_s)
    rstd_c, xhat_c = normalize(h_c, total[:, 2:3], total[:, 3:4], width_c)

    for q in dp_peers:
        arrived(rb.at[q], rb_recv.at[q], (e, q, r))
    pieces = [rb[o].astype(jnp.float32) for o in range(n_dp)]
    for i in range(slots):
        chosen = pieces[0]
        for o in range(1, n_dp):
            chosen = jnp.where(own_s[0, i] == o, pieces[o], chosen)
        dy[i * depth : (i + 1) * depth, :] = chosen
    loads[8].wait()
    loads[9].wait()
    joint[...] = jnp.zeros_like(joint)
    joint[:, 0:cs] = dy[:, 0:cs] * gs_v[...].reshape(1, cs)
    joint[:, lo : lo + cn] = dy[:, lo : lo + cn] * gc_v[...].reshape(1, cn)
    gy_s, gy_c = joint[:, 0:lo], joint[:, lo:]
    st2[e] = four((gy_s, gy_s * xhat_s, gy_c, gy_c * xhat_c))
    for k, p in enumerate(enc_peers):
        send(st2.at[e], st2.at[e], st2_send.at[k], st2_recv.at[e], (p, d, r))

    for k, q in enumerate(dp_peers):
        at = q * n_rep + r
        arrived(fa.at[at], fa_recv.at[at], (e, q, r))
        send(fa.at[at], fa.at[at], fwd_send.at[k], fa_recv.at[at], (e, d, partner))

    for p in enc_peers:
        arrived(st2.at[p], st2_recv.at[p], (p, d, r))
    later = st2[0]
    for i in range(1, n_enc):
        later += st2[i]
    mean_s, prod_s = later[:, 0:1] / width_s, later[:, 1:2] / width_s
    mean_c, prod_c = later[:, 2:3] / width_c, later[:, 3:4] / width_c
    os_ref[...] = (rstd_s * (gy_s - mean_s - xhat_s * prod_s))[:, 0:cs].astype(os_ref.dtype)
    oc_ref[...] = (rstd_c * (gy_c - mean_c - xhat_c * prod_c))[:, 0:cn].astype(oc_ref.dtype)

    for q in dp_peers:
        for s in range(n_rep):
            at = q * n_rep + s
            arrived(cc.at[at], cc_recv.at[at], (e, q, s))
        other = q * n_rep + partner
        arrived(fa.at[other], fa_recv.at[other], (e, d, partner))
    beside = d * n_rep + partner
    arrived(cc.at[beside], cc_recv.at[beside], (e, d, partner))
    arrived(fa.at[beside], fa_recv.at[beside], (e, d, partner))

    for copy in sent:
        copy.wait_send()


def weight_kernel(
    scale, fa, cc, os_v, oc_v, gws_hbm, gwc_hbm, os_hbm, oc_hbm, gws_v, gwc_v, out_sem
):
    tokens = cc.shape[0] * cc.shape[1]
    cs, cn = gws_v.shape[0], gwc_v.shape[1]
    lo = round_up(cs)
    stores = [
        pltpu.make_async_copy(os_v, os_hbm, out_sem.at[0]),
        pltpu.make_async_copy(oc_v, oc_hbm, out_sem.at[1]),
        pltpu.make_async_copy(gws_v, gws_hbm, out_sem.at[2]),
        pltpu.make_async_copy(gwc_v, gwc_hbm, out_sem.at[3]),
    ]
    stores[0].start()
    stores[1].start()
    cot_all = cc[...].reshape(tokens, cc.shape[2])
    over_rows = (((0,), (0,)), ((), ()))
    gws_v[...] = (
        lax.dot_general(
            fa[:, :, 0:lo].reshape(tokens, lo),
            cot_all,
            over_rows,
            preferred_element_type=jnp.float32,
        )[0:cs, :]
        * scale
    )
    stores[2].start()
    gwc_v[...] = (
        lax.dot_general(
            cot_all,
            fa[:, :, lo:].reshape(tokens, fa.shape[2] - lo),
            over_rows,
            preferred_element_type=jnp.float32,
        )[:, 0:cn]
        * scale
    )
    stores[3].start()
    for store in stores:
        store.wait()


def gather_shards(
    feat_sig,
    feat_cnx,
    cotangent,
    w_sig,
    w_cnx,
    lengths,
    enc_of,
    owner_of,
    pre_sig,
    pre_cnx,
    gain_sig,
    gain_cnx,
):
    n_enc, n_dp, n_rep = (lax.axis_size(axis) for axis in ("enc", "dp", "rep"))
    slots = lengths.shape[1]
    rows, chunk = cotangent.shape
    depth = rows // slots
    cs, cn = feat_sig.shape[1], feat_cnx.shape[1]
    whole = w_sig.shape[0]
    owners = n_dp * n_rep
    block = whole // owners
    joint = round_up(cs) + round_up(cn)
    bf16, f32 = jnp.bfloat16, jnp.float32
    dma = pltpu.SemaphoreType.DMA
    scratch = [
        pltpu.SMEM((1, slots), jnp.int32),
        pltpu.SMEM((1, slots), jnp.int32),
        pltpu.SMEM((1, slots), jnp.int32),
        pltpu.VMEM((rows, cs), bf16),
        pltpu.VMEM((rows, cn), bf16),
        pltpu.VMEM((rows, cs), bf16),
        pltpu.VMEM((rows, cn), bf16),
        pltpu.VMEM((cs,), f32),
        pltpu.VMEM((cn,), f32),
        pltpu.VMEM((cs, whole), bf16),
        pltpu.VMEM((whole, cn), bf16),
        pltpu.VMEM((n_enc, rows, chunk), bf16),
        pltpu.VMEM((n_dp, depth, joint), bf16),
        pltpu.VMEM((n_dp, depth, joint), bf16),
        pltpu.VMEM((n_enc, rows, LANES), f32),
        pltpu.VMEM((n_enc, rows, LANES), f32),
        pltpu.VMEM((rows, joint), f32),
        pltpu.VMEM((rows, joint), f32),
        pltpu.VMEM((rows, joint), f32),
        dma((10,)),
        dma((2 * n_enc,)),
        dma((n_enc,)),
        dma((n_enc,)),
        dma((n_dp,)),
        dma((owners,)),
        dma((n_dp,)),
        dma((owners,)),
        dma((owners,)),
        dma((n_dp,)),
        dma((n_dp,)),
        dma((n_enc,)),
        dma((n_enc,)),
        dma((n_enc,)),
        dma((n_enc,)),
    ]
    hbm = pl.BlockSpec(memory_space=pltpu.HBM)
    vmem = pl.BlockSpec(memory_space=pltpu.VMEM)
    parts = pl.pallas_call(
        functools.partial(fused_kernel, (n_enc, n_dp, n_rep, slots, depth)),
        out_shape=(
            pltpu.VMEM((owners, rows, joint), bf16),
            pltpu.VMEM((owners, rows, block), bf16),
            pltpu.VMEM((rows, cs), bf16),
            pltpu.VMEM((rows, cn), bf16),
        ),
        in_specs=[hbm] * 12,
        out_specs=(vmem,) * 4,
        scratch_shapes=scratch,
        compiler_params=pltpu.CompilerParams(
            collective_id=0, has_side_effects=True, vmem_limit_bytes=VMEM_BYTES
        ),
        cost_estimate=pl.CostEstimate(
            flops=2 * rows * whole * (cs + cn),
            bytes_accessed=2 * whole * (cs + cn),
            transcendentals=2 * rows,
        ),
    )(
        lengths,
        enc_of,
        owner_of,
        cotangent,
        feat_sig,
        feat_cnx,
        pre_sig,
        pre_cnx,
        gain_sig,
        gain_cnx,
        w_sig.T,
        w_cnx,
    )
    grad_w_sig, *rest = pl.pallas_call(
        functools.partial(weight_kernel, 1.0 / math.sqrt(owners * rows)),
        out_shape=(
            jax.ShapeDtypeStruct((cs, block), f32),
            jax.ShapeDtypeStruct((block, cn), f32),
            jax.ShapeDtypeStruct((rows, cs), bf16),
            jax.ShapeDtypeStruct((rows, cn), bf16),
        ),
        in_specs=[vmem] * 4,
        out_specs=(hbm,) * 4,
        scratch_shapes=[pltpu.VMEM((cs, block), f32), pltpu.VMEM((block, cn), f32), dma((4,))],
        compiler_params=pltpu.CompilerParams(vmem_limit_bytes=VMEM_BYTES // 4),
        cost_estimate=pl.CostEstimate(
            flops=2 * rows * owners * block * (cs + cn),
            bytes_accessed=4 * block * (cs + cn),
            transcendentals=0,
        ),
    )(*parts)
    return (grad_w_sig.T, *rest)


def shards(feat_sig, feat_cnx, cotangent, w_sig, *others):
    n_enc, n_dp, n_rep = (lax.axis_size(axis) for axis in ("enc", "dp", "rep"))
    rows, chunk = cotangent.shape
    owners = n_dp * n_rep
    whole = w_sig.shape[0]
    gathered = owners * rows * (feat_sig.shape[1] + feat_cnx.shape[1]) * 2
    fits = gathered <= GATHER_BYTES and n_rep == 2 and rows % 16 == 0
    fits = fits and others[1].shape[1] == n_dp and whole % (owners * LANES) == 0
    fits = fits and chunk % (whole // owners) == 0
    form = gather_shards if fits else partial_sum_shards
    return form(feat_sig, feat_cnx, cotangent, w_sig, *others)


def solution(mesh):
    in_specs = (
        P(("dp", "rep"), "enc"),
        P(("dp", "rep"), "enc"),
        P(("dp", "rep"), "enc"),
        P(None, "enc"),
        P(None, "enc"),
        P(("dp", "rep"), None),
        P(("dp", "rep"), None),
        P(("dp", "rep"), None),
        P(("dp", "rep"), "enc"),
        P(("dp", "rep"), "enc"),
        P("enc"),
        P("enc"),
    )
    out_specs = (
        P(("dp", "rep"), "enc"),
        P(("dp", "rep"), "enc"),
        P(("dp", "rep"), "enc"),
        P(("dp", "rep"), "enc"),
    )
    return jax.shard_map(shards, mesh=mesh, in_specs=in_specs, out_specs=out_specs, check_vma=False)
```

```python
import functools
import math

import jax
import jax.numpy as jnp
from jax import lax
from jax.experimental import pallas as pl
from jax.experimental.pallas import tpu as pltpu
from jax.sharding import PartitionSpec as P

EPS = 1e-06
LANES = 128
GATHER_BYTES = 4 * 1024 * 1024
VMEM_BYTES = 58 * 1024 * 1024
MESH = pl.DeviceIdType.MESH


def row_statistics_pair(row_height, sum_h, sum_hh, feature_width):
    hidden_mean = sum_h[:, None] / feature_width
    var_h = sum_hh[:, None] / feature_width - hidden_mean * hidden_mean
    inverse_deviation = lax.rsqrt(var_h + EPS)
    return (hidden_mean, inverse_deviation, (row_height - hidden_mean) * inverse_deviation)


def partial_sum_shards(
    feat_sig,
    feat_cnx,
    cotangent,
    w_sig,
    w_cnx,
    lengths,
    enc_of,
    owner_of,
    pre_sig,
    pre_cnx,
    gain_sig,
    gain_cnx,
):
    slots = lengths.shape[1]
    rows = cotangent.shape[0]
    depth = rows // slots
    spots = lax.broadcasted_iota(jnp.int32, (slots, depth), 1)
    live = (spots < lengths[0][:, None]).reshape(rows, 1)
    masked = jnp.where(live, cotangent, jnp.zeros_like(cotangent))
    full_grad = lax.all_gather(masked, "enc", axis=1, tiled=True)
    back_sig = jnp.dot(full_grad, w_sig, preferred_element_type=jnp.float32).astype(jnp.bfloat16)
    back_cnx = jnp.dot(full_grad, w_cnx, preferred_element_type=jnp.float32).astype(jnp.bfloat16)
    inverse = jnp.argsort(enc_of[0])
    send_sig = jnp.take(back_sig.reshape(slots, depth, back_sig.shape[1]), inverse, axis=0)
    send_cnx = jnp.take(back_cnx.reshape(slots, depth, back_cnx.shape[1]), inverse, axis=0)
    recv_sig, recv_cnx = (
        lax.all_to_all(send_sig, "dp", split_axis=0, concat_axis=0, tiled=True),
        lax.all_to_all(send_cnx, "dp", split_axis=0, concat_axis=0, tiled=True),
    )
    sources = owner_of[0]
    dy_sig = jnp.take(recv_sig, sources, axis=0).reshape(rows, recv_sig.shape[2])
    dy_cnx = jnp.take(recv_cnx, sources, axis=0).reshape(rows, recv_cnx.shape[2])
    enc_count = lax.axis_size("enc")
    siglip_width = gain_sig.shape[0] * enc_count
    convnext_width = gain_cnx.shape[0] * enc_count
    siglip_height = pre_sig.astype(jnp.float32)
    convnext_height = pre_cnx.astype(jnp.float32)
    siglip_scaled_gradient = dy_sig.astype(jnp.float32) * gain_sig
    convnext_scaled_gradient = dy_cnx.astype(jnp.float32) * gain_cnx
    row_totals = lax.psum(
        (
            jnp.sum(siglip_height, axis=1),
            jnp.sum(siglip_height * siglip_height, axis=1),
            jnp.sum(convnext_height, axis=1),
            jnp.sum(convnext_height * convnext_height, axis=1),
        ),
        "enc",
    )
    siglip_mean, siglip_inverse_deviation, siglip_normalized = row_statistics_pair(
        siglip_height, row_totals[0], row_totals[1], siglip_width
    )
    convnext_mean, convnext_inverse_deviation, convnext_normalized = row_statistics_pair(
        convnext_height, row_totals[2], row_totals[3], convnext_width
    )
    later = lax.psum(
        (
            jnp.sum(siglip_scaled_gradient, axis=1),
            jnp.sum(siglip_scaled_gradient * siglip_normalized, axis=1),
            jnp.sum(convnext_scaled_gradient, axis=1),
            jnp.sum(convnext_scaled_gradient * convnext_normalized, axis=1),
        ),
        "enc",
    )
    siglip_gradient_mean = later[0][:, None] / siglip_width
    siglip_product_mean = later[1][:, None] / siglip_width
    convnext_gradient_mean = later[2][:, None] / convnext_width
    convnext_product_mean = later[3][:, None] / convnext_width
    gradient_before_siglip = (
        siglip_inverse_deviation
        * (siglip_scaled_gradient - siglip_gradient_mean - siglip_normalized * siglip_product_mean)
    ).astype(jnp.bfloat16)
    gradient_before_convnext = (
        convnext_inverse_deviation
        * (
            convnext_scaled_gradient
            - convnext_gradient_mean
            - convnext_normalized * convnext_product_mean
        )
    ).astype(jnp.bfloat16)
    dp_count = lax.axis_size("dp")
    rep_count = lax.axis_size("rep")
    scale = 1.0 / math.sqrt(rows * dp_count * rep_count)
    split = feat_sig.shape[1]
    features = jnp.concatenate([feat_sig, feat_cnx], axis=1)
    summed = lax.psum_scatter(
        lax.dot_general(
            full_grad, features, (((0,), (0,)), ((), ())), preferred_element_type=jnp.float32
        ),
        ("dp", "rep"),
        scatter_dimension=0,
        tiled=True,
    )
    summed = summed * scale
    return (summed[:, :split], summed[:, split:], gradient_before_siglip, gradient_before_convnext)


def round_up(width):
    return -(-width // LANES) * LANES


def fused_kernel(
    sizes,
    lengths_hbm,
    enc_of_hbm,
    owner_of_hbm,
    cot_hbm,
    fs_hbm,
    fc_hbm,
    ps_hbm,
    pc_hbm,
    gs_hbm,
    gc_hbm,
    ws_hbm,
    wc_hbm,
    fa,
    cc,
    os_ref,
    oc_ref,
    len_s,
    enc_s,
    own_s,
    fs_v,
    fc_v,
    ps_v,
    pc_v,
    gs_v,
    gc_v,
    ws_v,
    wc_v,
    fg,
    sb,
    rb,
    st1,
    st2,
    joint,
    height,
    dy,
    local_sem,
    w_sem,
    fg_send,
    fg_recv,
    fa_send,
    fa_recv,
    relay_send,
    line_send,
    line_recv,
    fwd_send,
    cc_send,
    cc_recv,
    rb_send,
    rb_recv,
    st1_send,
    st1_recv,
    st2_send,
    st2_recv,
):
    n_enc, n_dp, n_rep, slots, depth = sizes
    rows = slots * depth
    e, d, r = lax.axis_index("enc"), lax.axis_index("dp"), lax.axis_index("rep")
    chunk = cot_hbm.shape[1]
    cs, cn = fs_v.shape[1], fc_v.shape[1]
    lo = round_up(cs)
    block = cc.shape[2]
    per = chunk // block
    width_s, width_c = cs * n_enc, cn * n_enc
    b = d * n_rep + r
    enc_peers = [lax.rem(e + k, n_enc) for k in range(1, n_enc)]
    dp_peers = [lax.rem(d + k, n_dp) for k in range(1, n_dp)]
    partner = 1 - r
    half = n_dp // 2
    side = d // half
    mates = [side * half + lax.rem(d + k, half) for k in range(1, half)]
    crossed = [(1 - side) * half + k for k in range(half)]
    gateway = half - 1 + side
    far_gateway = half - side
    is_gateway = d == gateway
    is_sender = d == e

    barrier = pltpu.get_barrier_semaphore()
    for p in enc_peers:
        pl.semaphore_signal(barrier, inc=1, device_id=(p, d, r), device_id_type=MESH)
    for q in dp_peers:
        for s in range(n_rep):
            pl.semaphore_signal(barrier, inc=1, device_id=(e, q, s), device_id_type=MESH)
    pl.semaphore_signal(barrier, inc=1, device_id=(e, d, partner), device_id_type=MESH)

    pairs = (
        (lengths_hbm, len_s),
        (enc_of_hbm, enc_s),
        (owner_of_hbm, own_s),
        (cot_hbm, fg.at[e]),
        (fs_hbm, fs_v),
        (fc_hbm, fc_v),
        (ps_hbm, ps_v),
        (pc_hbm, pc_v),
        (gs_hbm, gs_v),
        (gc_hbm, gc_v),
    )
    loads = [
        pltpu.make_async_copy(source, target, local_sem.at[i])
        for i, (source, target) in enumerate(pairs)
    ]
    for load in loads:
        load.start()
    w_loads = []
    for k in range(n_enc):
        p = lax.rem(e + k, n_enc)
        at = pl.ds(pl.multiple_of(p * chunk, chunk), chunk)
        pair = (
            pltpu.make_async_copy(ws_hbm.at[:, at], ws_v.at[:, at], w_sem.at[2 * k]),
            pltpu.make_async_copy(wc_hbm.at[at], wc_v.at[at], w_sem.at[2 * k + 1]),
        )
        for load in pair:
            load.start()
        w_loads.append(pair)

    pl.semaphore_wait(barrier, n_enc - 1 + n_dp * n_rep - 1)

    sent = []

    def send(src, dst, send_sem, recv_sem, device):
        copy = pltpu.make_async_remote_copy(
            src_ref=src,
            dst_ref=dst,
            send_sem=send_sem,
            recv_sem=recv_sem,
            device_id=device,
            device_id_type=MESH,
        )
        copy.start()
        sent.append(copy)

    def arrived(dst, recv_sem, device):
        pltpu.make_async_remote_copy(
            src_ref=dst,
            dst_ref=dst,
            send_sem=recv_sem,
            recv_sem=recv_sem,
            device_id=device,
            device_id_type=MESH,
        ).wait_recv()

    for k, p in enumerate(enc_peers):
        send(cot_hbm, fg.at[e], fg_send.at[k], fg_recv.at[e], (p, d, r))

    for i in (0, 1, 2, 4, 5):
        loads[i].wait()
    row = lax.broadcasted_iota(jnp.int32, (rows, 1), 0)
    live = jnp.zeros((rows, 1), jnp.float32)
    for j in range(slots):
        spot = row - j * depth
        live = jnp.where((spot >= 0) & (spot < len_s[0, j]), 1.0, live)
    fa[b] = jnp.zeros_like(fa[b])
    fa[b, :, 0:cs] = (fs_v[...].astype(jnp.float32) * live).astype(jnp.bfloat16)
    fa[b, :, lo : lo + cn] = (fc_v[...].astype(jnp.float32) * live).astype(jnp.bfloat16)
    send(fa.at[b], fa.at[b], fa_send.at[0], fa_recv.at[b], (e, far_gateway, r))
    for k, q in enumerate(mates):
        send(fa.at[b], fa.at[b], fa_send.at[2 + k], fa_recv.at[b], (e, q, r))
    send(fa.at[b], fa.at[b], fa_send.at[1], fa_recv.at[b], (e, d, partner))

    loads[6].wait()
    loads[7].wait()
    height[...] = jnp.zeros_like(height)
    height[:, 0:cs] = ps_v[...].astype(jnp.float32)
    height[:, lo : lo + cn] = pc_v[...].astype(jnp.float32)
    h_s, h_c = height[:, 0:lo], height[:, lo:]
    lane = lax.broadcasted_iota(jnp.int32, (rows, LANES), 1)

    def four(values):
        sums = [jnp.sum(v, axis=1, keepdims=True) for v in values]
        packed = jnp.zeros((rows, LANES), jnp.float32)
        for i, total in enumerate(sums):
            packed = jnp.where(lane == i, total, packed)
        return packed

    st1[e] = four((h_s, h_s * h_s, h_c, h_c * h_c))
    for k, p in enumerate(enc_peers):
        send(st1.at[e], st1.at[e], st1_send.at[k], st1_recv.at[e], (p, d, r))

    acc_s = jnp.zeros((rows, cs), jnp.float32)
    acc_c = jnp.zeros((rows, cn), jnp.float32)
    for k in range(n_enc):
        p = lax.rem(e + k, n_enc)
        at = pl.ds(pl.multiple_of(p * chunk, chunk), chunk)
        for load in w_loads[k]:
            load.wait()
        if k == 0:
            loads[3].wait()
        else:
            arrived(fg.at[p], fg_recv.at[p], (p, d, r))
        part = fg[p]
        acc_s += lax.dot_general(
            part, ws_v[:, at], (((1,), (1,)), ((), ())), preferred_element_type=jnp.float32
        )
        acc_c += jnp.dot(part, wc_v[at, :], preferred_element_type=jnp.float32)
    joint[...] = jnp.zeros_like(joint)
    joint[:, 0:cs] = acc_s * live
    joint[:, lo : lo + cn] = acc_c * live
    slices = [joint[j * depth : (j + 1) * depth, :] for j in range(slots)]
    for i in range(n_dp):
        chosen = slices[0]
        for j in range(1, slots):
            chosen = jnp.where(enc_s[0, j] == i, slices[j], chosen)
        sb[i] = chosen.astype(jnp.bfloat16)
    rb[d] = sb[d]
    for k, q in enumerate(dp_peers):
        send(sb.at[q], rb.at[d], rb_send.at[k], rb_recv.at[d], (e, q, r))

    def remote(src, dst, send_sem, recv_sem, device):
        return pltpu.make_async_remote_copy(
            src_ref=src,
            dst_ref=dst,
            send_sem=send_sem,
            recv_sem=recv_sem,
            device_id=device,
            device_id_type=MESH,
        )

    def my_block(q, s):
        first = q * n_rep + s
        at = pl.ds(pl.multiple_of(lax.rem(first, per) * block, block), block)
        return fg.at[first // per, :, at]

    def line_blocks():
        targets = [(d, partner)] + [(q, s) for q in dp_peers for s in range(n_rep)]
        return [
            remote(my_block(q, s), cc.at[b], cc_send.at[i], cc_recv.at[b], (e, q, s))
            for i, (q, s) in enumerate(targets)
        ]

    def relay():
        copies = []
        for k, q in enumerate(crossed):
            at = q * n_rep + r
            for m, mate in enumerate(mates):
                sem = relay_send.at[k * (half - 1) + m]
                copies.append(remote(fa.at[at], fa.at[at], sem, fa_recv.at[at], (e, mate, r)))
        return copies

    @pl.when(is_sender)
    def _():
        cc[b] = my_block(d, r)[...]
        for copy in line_blocks():
            copy.start()

    for p in enc_peers:
        arrived(st1.at[p], st1_recv.at[p], (p, d, r))
    total = st1[0]
    for i in range(1, n_enc):
        total += st1[i]

    def normalize(h, sum_h, sum_hh, width):
        mean = sum_h / width
        rstd = lax.rsqrt(sum_hh / width - mean * mean + EPS)
        return rstd, (h - mean) * rstd

    rstd_s, xhat_s = normalize(h_s, total[:, 0:1], total[:, 1:2], width_s)
    rstd_c, xhat_c = normalize(h_c, total[:, 2:3], total[:, 3:4], width_c)

    @pl.when(is_gateway)
    def _():
        for q in crossed:
            arrived(fa.at[q * n_rep + r], fa_recv.at[q * n_rep + r], (e, q, r))
        for copy in relay():
            copy.start()

    for q in dp_peers:
        arrived(rb.at[q], rb_recv.at[q], (e, q, r))
    pieces = [rb[o].astype(jnp.float32) for o in range(n_dp)]
    for i in range(slots):
        chosen = pieces[0]
        for o in range(1, n_dp):
            chosen = jnp.where(own_s[0, i] == o, pieces[o], chosen)
        dy[i * depth : (i + 1) * depth, :] = chosen
    loads[8].wait()
    loads[9].wait()
    joint[...] = jnp.zeros_like(joint)
    joint[:, 0:cs] = dy[:, 0:cs] * gs_v[...].reshape(1, cs)
    joint[:, lo : lo + cn] = dy[:, lo : lo + cn] * gc_v[...].reshape(1, cn)
    gy_s, gy_c = joint[:, 0:lo], joint[:, lo:]
    st2[e] = four((gy_s, gy_s * xhat_s, gy_c, gy_c * xhat_c))
    for k, p in enumerate(enc_peers):
        send(st2.at[e], st2.at[e], st2_send.at[k], st2_recv.at[e], (p, d, r))

    @pl.when(is_sender)
    def _():
        beside = e * n_rep + partner
        arrived(cc.at[beside], cc_recv.at[beside], (e, d, partner))

    @pl.when(jnp.logical_not(is_sender))
    def _():
        for s in range(n_rep):
            at = e * n_rep + s
            arrived(cc.at[at], cc_recv.at[at], (e, e, s))

    def line(p):
        return cc.at[pl.ds(p * n_rep, n_rep)]

    for k, p in enumerate(enc_peers):
        send(line(e), line(e), line_send.at[k], line_recv.at[e], (p, d, r))

    for k, q in enumerate(mates):
        at = q * n_rep + r
        arrived(fa.at[at], fa_recv.at[at], (e, q, r))
        send(fa.at[at], fa.at[at], fwd_send.at[half + k], fa_recv.at[at], (e, d, partner))

    @pl.when(jnp.logical_not(is_gateway))
    def _():
        for q in crossed:
            arrived(fa.at[q * n_rep + r], fa_recv.at[q * n_rep + r], (e, gateway, r))

    for k, q in enumerate(crossed):
        at = q * n_rep + r
        send(fa.at[at], fa.at[at], fwd_send.at[k], fa_recv.at[at], (e, d, partner))

    for p in enc_peers:
        arrived(st2.at[p], st2_recv.at[p], (p, d, r))
    later = st2[0]
    for i in range(1, n_enc):
        later += st2[i]
    mean_s, prod_s = later[:, 0:1] / width_s, later[:, 1:2] / width_s
    mean_c, prod_c = later[:, 2:3] / width_c, later[:, 3:4] / width_c
    os_ref[...] = (rstd_s * (gy_s - mean_s - xhat_s * prod_s))[:, 0:cs].astype(os_ref.dtype)
    oc_ref[...] = (rstd_c * (gy_c - mean_c - xhat_c * prod_c))[:, 0:cn].astype(oc_ref.dtype)

    for p in enc_peers:
        arrived(line(p), line_recv.at[p], (p, d, r))
    for q in [d] + dp_peers:
        other = q * n_rep + partner
        arrived(fa.at[other], fa_recv.at[other], (e, d, partner))

    for copy in sent:
        copy.wait_send()

    @pl.when(is_sender)
    def _():
        for copy in line_blocks():
            copy.wait_send()

    @pl.when(is_gateway)
    def _():
        for copy in relay():
            copy.wait_send()


def weight_kernel(
    scale, fa, cc, os_v, oc_v, gws_hbm, gwc_hbm, os_hbm, oc_hbm, gws_v, gwc_v, out_sem
):
    tokens = cc.shape[0] * cc.shape[1]
    cs, cn = gws_v.shape[0], gwc_v.shape[1]
    lo = round_up(cs)
    stores = [
        pltpu.make_async_copy(os_v, os_hbm, out_sem.at[0]),
        pltpu.make_async_copy(oc_v, oc_hbm, out_sem.at[1]),
        pltpu.make_async_copy(gws_v, gws_hbm, out_sem.at[2]),
        pltpu.make_async_copy(gwc_v, gwc_hbm, out_sem.at[3]),
    ]
    stores[0].start()
    stores[1].start()
    cot_all = cc[...].reshape(tokens, cc.shape[2])
    over_rows = (((0,), (0,)), ((), ()))
    gws_v[...] = (
        lax.dot_general(
            fa[:, :, 0:lo].reshape(tokens, lo),
            cot_all,
            over_rows,
            preferred_element_type=jnp.float32,
        )[0:cs, :]
        * scale
    )
    stores[2].start()
    gwc_v[...] = (
        lax.dot_general(
            cot_all,
            fa[:, :, lo:].reshape(tokens, fa.shape[2] - lo),
            over_rows,
            preferred_element_type=jnp.float32,
        )[:, 0:cn]
        * scale
    )
    stores[3].start()
    for store in stores:
        store.wait()


def gather_shards(
    feat_sig,
    feat_cnx,
    cotangent,
    w_sig,
    w_cnx,
    lengths,
    enc_of,
    owner_of,
    pre_sig,
    pre_cnx,
    gain_sig,
    gain_cnx,
):
    n_enc, n_dp, n_rep = (lax.axis_size(axis) for axis in ("enc", "dp", "rep"))
    slots = lengths.shape[1]
    rows, chunk = cotangent.shape
    depth = rows // slots
    cs, cn = feat_sig.shape[1], feat_cnx.shape[1]
    whole = w_sig.shape[0]
    owners = n_dp * n_rep
    block = whole // owners
    joint = round_up(cs) + round_up(cn)
    bf16, f32 = jnp.bfloat16, jnp.float32
    dma = pltpu.SemaphoreType.DMA
    scratch = [
        pltpu.SMEM((1, slots), jnp.int32),
        pltpu.SMEM((1, slots), jnp.int32),
        pltpu.SMEM((1, slots), jnp.int32),
        pltpu.VMEM((rows, cs), bf16),
        pltpu.VMEM((rows, cn), bf16),
        pltpu.VMEM((rows, cs), bf16),
        pltpu.VMEM((rows, cn), bf16),
        pltpu.VMEM((cs,), f32),
        pltpu.VMEM((cn,), f32),
        pltpu.VMEM((cs, whole), bf16),
        pltpu.VMEM((whole, cn), bf16),
        pltpu.VMEM((n_enc, rows, chunk), bf16),
        pltpu.VMEM((n_dp, depth, joint), bf16),
        pltpu.VMEM((n_dp, depth, joint), bf16),
        pltpu.VMEM((n_enc, rows, LANES), f32),
        pltpu.VMEM((n_enc, rows, LANES), f32),
        pltpu.VMEM((rows, joint), f32),
        pltpu.VMEM((rows, joint), f32),
        pltpu.VMEM((rows, joint), f32),
        dma((10,)),
        dma((2 * n_enc,)),
        dma((n_enc,)),
        dma((n_enc,)),
        dma((n_dp,)),
        dma((owners,)),
        dma((n_dp * n_dp,)),
        dma((n_enc,)),
        dma((n_enc,)),
        dma((n_dp,)),
        dma((owners,)),
        dma((owners,)),
        dma((n_dp,)),
        dma((n_dp,)),
        dma((n_enc,)),
        dma((n_enc,)),
        dma((n_enc,)),
        dma((n_enc,)),
    ]
    hbm = pl.BlockSpec(memory_space=pltpu.HBM)
    vmem = pl.BlockSpec(memory_space=pltpu.VMEM)
    parts = pl.pallas_call(
        functools.partial(fused_kernel, (n_enc, n_dp, n_rep, slots, depth)),
        out_shape=(
            pltpu.VMEM((owners, rows, joint), bf16),
            pltpu.VMEM((owners, rows, block), bf16),
            pltpu.VMEM((rows, cs), bf16),
            pltpu.VMEM((rows, cn), bf16),
        ),
        in_specs=[hbm] * 12,
        out_specs=(vmem,) * 4,
        scratch_shapes=scratch,
        compiler_params=pltpu.CompilerParams(
            collective_id=0, has_side_effects=True, vmem_limit_bytes=VMEM_BYTES
        ),
        cost_estimate=pl.CostEstimate(
            flops=2 * rows * whole * (cs + cn),
            bytes_accessed=2 * whole * (cs + cn),
            transcendentals=2 * rows,
        ),
    )(
        lengths,
        enc_of,
        owner_of,
        cotangent,
        feat_sig,
        feat_cnx,
        pre_sig,
        pre_cnx,
        gain_sig,
        gain_cnx,
        w_sig.T,
        w_cnx,
    )
    grad_w_sig, *rest = pl.pallas_call(
        functools.partial(weight_kernel, 1.0 / math.sqrt(owners * rows)),
        out_shape=(
            jax.ShapeDtypeStruct((cs, block), f32),
            jax.ShapeDtypeStruct((block, cn), f32),
            jax.ShapeDtypeStruct((rows, cs), bf16),
            jax.ShapeDtypeStruct((rows, cn), bf16),
        ),
        in_specs=[vmem] * 4,
        out_specs=(hbm,) * 4,
        scratch_shapes=[pltpu.VMEM((cs, block), f32), pltpu.VMEM((block, cn), f32), dma((4,))],
        compiler_params=pltpu.CompilerParams(vmem_limit_bytes=VMEM_BYTES // 4),
        cost_estimate=pl.CostEstimate(
            flops=2 * rows * owners * block * (cs + cn),
            bytes_accessed=4 * block * (cs + cn),
            transcendentals=0,
        ),
    )(*parts)
    return (grad_w_sig.T, *rest)


def shards(feat_sig, feat_cnx, cotangent, w_sig, *others):
    n_enc, n_dp, n_rep = (lax.axis_size(axis) for axis in ("enc", "dp", "rep"))
    rows, chunk = cotangent.shape
    owners = n_dp * n_rep
    whole = w_sig.shape[0]
    gathered = owners * rows * (feat_sig.shape[1] + feat_cnx.shape[1]) * 2
    fits = gathered <= GATHER_BYTES and n_rep == 2 and n_enc == n_dp and n_dp % 2 == 0 and rows % 16 == 0
    fits = fits and others[1].shape[1] == n_dp and whole % (owners * LANES) == 0
    fits = fits and chunk % (whole // owners) == 0
    form = gather_shards if fits else partial_sum_shards
    return form(feat_sig, feat_cnx, cotangent, w_sig, *others)


def solution(mesh):
    in_specs = (
        P(("dp", "rep"), "enc"),
        P(("dp", "rep"), "enc"),
        P(("dp", "rep"), "enc"),
        P(None, "enc"),
        P(None, "enc"),
        P(("dp", "rep"), None),
        P(("dp", "rep"), None),
        P(("dp", "rep"), None),
        P(("dp", "rep"), "enc"),
        P(("dp", "rep"), "enc"),
        P("enc"),
        P("enc"),
    )
    out_specs = (
        P(("dp", "rep"), "enc"),
        P(("dp", "rep"), "enc"),
        P(("dp", "rep"), "enc"),
        P(("dp", "rep"), "enc"),
    )
    return jax.shard_map(shards, mesh=mesh, in_specs=in_specs, out_specs=out_specs, check_vma=False)
```

```python
import functools
import math

import jax
import jax.numpy as jnp
from jax import lax
from jax.experimental import pallas as pl
from jax.experimental.pallas import tpu as pltpu
from jax.sharding import PartitionSpec as P

EPS = 1e-06
LANES = 128
GATHER_BYTES = 4 * 1024 * 1024
VMEM_BYTES = 58 * 1024 * 1024
MESH = pl.DeviceIdType.MESH


def row_statistics_pair(row_height, sum_h, sum_hh, feature_width):
    hidden_mean = sum_h[:, None] / feature_width
    var_h = sum_hh[:, None] / feature_width - hidden_mean * hidden_mean
    inverse_deviation = lax.rsqrt(var_h + EPS)
    return (hidden_mean, inverse_deviation, (row_height - hidden_mean) * inverse_deviation)


def partial_sum_shards(
    feat_sig,
    feat_cnx,
    cotangent,
    w_sig,
    w_cnx,
    lengths,
    enc_of,
    owner_of,
    pre_sig,
    pre_cnx,
    gain_sig,
    gain_cnx,
):
    slots = lengths.shape[1]
    rows = cotangent.shape[0]
    depth = rows // slots
    spots = lax.broadcasted_iota(jnp.int32, (slots, depth), 1)
    live = (spots < lengths[0][:, None]).reshape(rows, 1)
    masked = jnp.where(live, cotangent, jnp.zeros_like(cotangent))
    full_grad = lax.all_gather(masked, "enc", axis=1, tiled=True)
    back_sig = jnp.dot(full_grad, w_sig, preferred_element_type=jnp.float32).astype(jnp.bfloat16)
    back_cnx = jnp.dot(full_grad, w_cnx, preferred_element_type=jnp.float32).astype(jnp.bfloat16)
    inverse = jnp.argsort(enc_of[0])
    send_sig = jnp.take(back_sig.reshape(slots, depth, back_sig.shape[1]), inverse, axis=0)
    send_cnx = jnp.take(back_cnx.reshape(slots, depth, back_cnx.shape[1]), inverse, axis=0)
    recv_sig, recv_cnx = (
        lax.all_to_all(send_sig, "dp", split_axis=0, concat_axis=0, tiled=True),
        lax.all_to_all(send_cnx, "dp", split_axis=0, concat_axis=0, tiled=True),
    )
    sources = owner_of[0]
    dy_sig = jnp.take(recv_sig, sources, axis=0).reshape(rows, recv_sig.shape[2])
    dy_cnx = jnp.take(recv_cnx, sources, axis=0).reshape(rows, recv_cnx.shape[2])
    enc_count = lax.axis_size("enc")
    siglip_width = gain_sig.shape[0] * enc_count
    convnext_width = gain_cnx.shape[0] * enc_count
    siglip_height = pre_sig.astype(jnp.float32)
    convnext_height = pre_cnx.astype(jnp.float32)
    siglip_scaled_gradient = dy_sig.astype(jnp.float32) * gain_sig
    convnext_scaled_gradient = dy_cnx.astype(jnp.float32) * gain_cnx
    row_totals = lax.psum(
        (
            jnp.sum(siglip_height, axis=1),
            jnp.sum(siglip_height * siglip_height, axis=1),
            jnp.sum(convnext_height, axis=1),
            jnp.sum(convnext_height * convnext_height, axis=1),
        ),
        "enc",
    )
    siglip_mean, siglip_inverse_deviation, siglip_normalized = row_statistics_pair(
        siglip_height, row_totals[0], row_totals[1], siglip_width
    )
    convnext_mean, convnext_inverse_deviation, convnext_normalized = row_statistics_pair(
        convnext_height, row_totals[2], row_totals[3], convnext_width
    )
    later = lax.psum(
        (
            jnp.sum(siglip_scaled_gradient, axis=1),
            jnp.sum(siglip_scaled_gradient * siglip_normalized, axis=1),
            jnp.sum(convnext_scaled_gradient, axis=1),
            jnp.sum(convnext_scaled_gradient * convnext_normalized, axis=1),
        ),
        "enc",
    )
    siglip_gradient_mean = later[0][:, None] / siglip_width
    siglip_product_mean = later[1][:, None] / siglip_width
    convnext_gradient_mean = later[2][:, None] / convnext_width
    convnext_product_mean = later[3][:, None] / convnext_width
    gradient_before_siglip = (
        siglip_inverse_deviation
        * (siglip_scaled_gradient - siglip_gradient_mean - siglip_normalized * siglip_product_mean)
    ).astype(jnp.bfloat16)
    gradient_before_convnext = (
        convnext_inverse_deviation
        * (
            convnext_scaled_gradient
            - convnext_gradient_mean
            - convnext_normalized * convnext_product_mean
        )
    ).astype(jnp.bfloat16)
    dp_count = lax.axis_size("dp")
    rep_count = lax.axis_size("rep")
    scale = 1.0 / math.sqrt(rows * dp_count * rep_count)
    split = feat_sig.shape[1]
    features = jnp.concatenate([feat_sig, feat_cnx], axis=1)
    summed = lax.psum_scatter(
        lax.dot_general(
            full_grad, features, (((0,), (0,)), ((), ())), preferred_element_type=jnp.float32
        ),
        ("dp", "rep"),
        scatter_dimension=0,
        tiled=True,
    )
    summed = summed * scale
    return (summed[:, :split], summed[:, split:], gradient_before_siglip, gradient_before_convnext)


def round_up(width):
    return -(-width // LANES) * LANES


def fused_kernel(
    sizes,
    lengths_hbm,
    enc_of_hbm,
    owner_of_hbm,
    cot_hbm,
    fs_hbm,
    fc_hbm,
    ps_hbm,
    pc_hbm,
    gs_hbm,
    gc_hbm,
    ws_hbm,
    wc_hbm,
    fa,
    cc,
    os_ref,
    oc_ref,
    len_s,
    enc_s,
    own_s,
    cot_v,
    fs_v,
    fc_v,
    ps_v,
    pc_v,
    gs_v,
    gc_v,
    ws_v,
    wc_v,
    fg,
    sb,
    rb,
    st1,
    st2,
    joint,
    height,
    dy,
    local_sem,
    w_sem,
    fg_send,
    fg_recv,
    fa_send,
    fa_recv,
    fwd_send,
    cc_send,
    cc_recv,
    rb_send,
    rb_recv,
    st1_send,
    st1_recv,
    st2_send,
    st2_recv,
):
    n_enc, n_dp, n_rep, slots, depth = sizes
    rows = slots * depth
    e, d, r = lax.axis_index("enc"), lax.axis_index("dp"), lax.axis_index("rep")
    chunk = cot_v.shape[1]
    cs, cn = fs_v.shape[1], fc_v.shape[1]
    lo = round_up(cs)
    block = cc.shape[2]
    per = chunk // block
    width_s, width_c = cs * n_enc, cn * n_enc
    b = d * n_rep + r
    enc_peers = [lax.rem(e + k, n_enc) for k in range(1, n_enc)]
    dp_peers = [lax.rem(d + k, n_dp) for k in range(1, n_dp)]
    partner = 1 - r

    barrier = pltpu.get_barrier_semaphore()
    for p in enc_peers:
        pl.semaphore_signal(barrier, inc=1, device_id=(p, d, r), device_id_type=MESH)
    for q in dp_peers:
        for s in range(n_rep):
            pl.semaphore_signal(barrier, inc=1, device_id=(e, q, s), device_id_type=MESH)
    pl.semaphore_signal(barrier, inc=1, device_id=(e, d, partner), device_id_type=MESH)

    pairs = (
        (lengths_hbm, len_s),
        (enc_of_hbm, enc_s),
        (owner_of_hbm, own_s),
        (cot_hbm, cot_v),
        (fs_hbm, fs_v),
        (fc_hbm, fc_v),
        (ps_hbm, ps_v),
        (pc_hbm, pc_v),
        (gs_hbm, gs_v),
        (gc_hbm, gc_v),
    )
    loads = [
        pltpu.make_async_copy(source, target, local_sem.at[i])
        for i, (source, target) in enumerate(pairs)
    ]
    for load in loads:
        load.start()
    w_loads = []
    for k in range(n_enc):
        p = lax.rem(e + k, n_enc)
        at = pl.ds(pl.multiple_of(p * chunk, chunk), chunk)
        pair = (
            pltpu.make_async_copy(ws_hbm.at[:, at], ws_v.at[:, at], w_sem.at[2 * k]),
            pltpu.make_async_copy(wc_hbm.at[at], wc_v.at[at], w_sem.at[2 * k + 1]),
        )
        for load in pair:
            load.start()
        w_loads.append(pair)

    for i in range(4):
        loads[i].wait()
    row = lax.broadcasted_iota(jnp.int32, (rows, rows), 0)
    col = lax.broadcasted_iota(jnp.int32, (rows, rows), 1)
    same_spot = lax.rem(row, depth) == lax.rem(col, depth)
    pick = jnp.zeros((rows, rows), jnp.float32)
    for j in range(slots):
        taken = (col // depth == j) & (row // depth == enc_s[0, j])
        taken = taken & same_spot & (lax.rem(col, depth) < len_s[0, j])
        pick = jnp.where(taken, 1.0, pick)
    pick = pick.astype(jnp.bfloat16)
    mine = jnp.dot(pick, cot_v[...], preferred_element_type=jnp.float32).astype(jnp.bfloat16)
    fg[e] = mine

    pl.semaphore_wait(barrier, n_enc - 1 + n_dp * n_rep - 1)

    sent = []

    def send(src, dst, send_sem, recv_sem, device):
        copy = pltpu.make_async_remote_copy(
            src_ref=src,
            dst_ref=dst,
            send_sem=send_sem,
            recv_sem=recv_sem,
            device_id=device,
            device_id_type=MESH,
        )
        copy.start()
        sent.append(copy)

    def arrived(dst, recv_sem, device):
        pltpu.make_async_remote_copy(
            src_ref=dst,
            dst_ref=dst,
            send_sem=recv_sem,
            recv_sem=recv_sem,
            device_id=device,
            device_id_type=MESH,
        ).wait_recv()

    for k, p in enumerate(enc_peers):
        send(fg.at[e], fg.at[e], fg_send.at[k], fg_recv.at[e], (p, d, r))

    loads[4].wait()
    loads[5].wait()
    fa[b] = jnp.zeros_like(fa[b])
    fa[b, :, 0:cs] = jnp.dot(pick, fs_v[...], preferred_element_type=jnp.float32).astype(
        jnp.bfloat16
    )
    fa[b, :, lo : lo + cn] = jnp.dot(
        pick, fc_v[...], preferred_element_type=jnp.float32
    ).astype(jnp.bfloat16)
    for k, q in enumerate(dp_peers):
        send(fa.at[b], fa.at[b], fa_send.at[k], fa_recv.at[b], (e, q, r))
    send(fa.at[b], fa.at[b], fa_send.at[n_dp - 1], fa_recv.at[b], (e, d, partner))

    loads[6].wait()
    loads[7].wait()
    height[...] = jnp.zeros_like(height)
    height[:, 0:cs] = ps_v[...].astype(jnp.float32)
    height[:, lo : lo + cn] = pc_v[...].astype(jnp.float32)
    h_s, h_c = height[:, 0:lo], height[:, lo:]
    lane = lax.broadcasted_iota(jnp.int32, (rows, LANES), 1)

    def four(values):
        sums = [jnp.sum(v, axis=1, keepdims=True) for v in values]
        packed = jnp.zeros((rows, LANES), jnp.float32)
        for i, total in enumerate(sums):
            packed = jnp.where(lane == i, total, packed)
        return packed

    st1[e] = four((h_s, h_s * h_s, h_c, h_c * h_c))
    for k, p in enumerate(enc_peers):
        send(st1.at[e], st1.at[e], st1_send.at[k], st1_recv.at[e], (p, d, r))

    acc_s = jnp.zeros((cs, rows), jnp.float32)
    acc_c = jnp.zeros((rows, cn), jnp.float32)
    for k in range(n_enc):
        p = lax.rem(e + k, n_enc)
        at = pl.ds(pl.multiple_of(p * chunk, chunk), chunk)
        for load in w_loads[k]:
            load.wait()
        if k > 0:
            arrived(fg.at[p], fg_recv.at[p], (p, d, r))
        part = fg[p]
        acc_s += lax.dot_general(
            ws_v[:, at], part, (((1,), (1,)), ((), ())), preferred_element_type=jnp.float32
        )
        acc_c += jnp.dot(part, wc_v[at, :], preferred_element_type=jnp.float32)
    joint[...] = jnp.zeros_like(joint)
    joint[:, 0:cs] = acc_s.T
    joint[:, lo : lo + cn] = acc_c
    for i in range(slots):
        sb[i] = joint[i * depth : (i + 1) * depth, :].astype(jnp.bfloat16)
    rb[d] = sb[d]
    for k, q in enumerate(dp_peers):
        send(sb.at[q], rb.at[d], rb_send.at[k], rb_recv.at[d], (e, q, r))

    def my_block(q, s):
        first = q * n_rep + s
        return fg.at[first // per, :, pl.ds(pl.multiple_of(lax.rem(first, per) * block, block), block)]

    cc[b] = my_block(d, r)[...]
    count = 0
    for q in dp_peers:
        for s in range(n_rep):
            send(my_block(q, s), cc.at[b], cc_send.at[count], cc_recv.at[b], (e, q, s))
            count += 1
    send(my_block(d, partner), cc.at[b], cc_send.at[count], cc_recv.at[b], (e, d, partner))

    for p in enc_peers:
        arrived(st1.at[p], st1_recv.at[p], (p, d, r))
    total = st1[0]
    for i in range(1, n_enc):
        total += st1[i]

    def normalize(h, sum_h, sum_hh, width):
        mean = sum_h / width
        rstd = lax.rsqrt(sum_hh / width - mean * mean + EPS)
        return rstd, (h - mean) * rstd

    rstd_s, xhat_s = normalize(h_s, total[:, 0:1], total[:, 1:2], width_s)
    rstd_c, xhat_c = normalize(h_c, total[:, 2:3], total[:, 3:4], width_c)

    for k, q in enumerate(dp_peers):
        at = q * n_rep + r
        arrived(fa.at[at], fa_recv.at[at], (e, q, r))
        send(fa.at[at], fa.at[at], fwd_send.at[k], fa_recv.at[at], (e, d, partner))

    for q in dp_peers:
        arrived(rb.at[q], rb_recv.at[q], (e, q, r))
    pieces = [rb[o].astype(jnp.float32) for o in range(n_dp)]
    for i in range(slots):
        chosen = pieces[0]
        for o in range(1, n_dp):
            chosen = jnp.where(own_s[0, i] == o, pieces[o], chosen)
        dy[i * depth : (i + 1) * depth, :] = chosen
    loads[8].wait()
    loads[9].wait()
    joint[...] = jnp.zeros_like(joint)
    joint[:, 0:cs] = dy[:, 0:cs] * gs_v[...].reshape(1, cs)
    joint[:, lo : lo + cn] = dy[:, lo : lo + cn] * gc_v[...].reshape(1, cn)
    gy_s, gy_c = joint[:, 0:lo], joint[:, lo:]
    st2[e] = four((gy_s, gy_s * xhat_s, gy_c, gy_c * xhat_c))
    for k, p in enumerate(enc_peers):
        send(st2.at[e], st2.at[e], st2_send.at[k], st2_recv.at[e], (p, d, r))

    for p in enc_peers:
        arrived(st2.at[p], st2_recv.at[p], (p, d, r))
    later = st2[0]
    for i in range(1, n_enc):
        later += st2[i]
    mean_s, prod_s = later[:, 0:1] / width_s, later[:, 1:2] / width_s
    mean_c, prod_c = later[:, 2:3] / width_c, later[:, 3:4] / width_c
    os_ref[...] = (rstd_s * (gy_s - mean_s - xhat_s * prod_s))[:, 0:cs].astype(os_ref.dtype)
    oc_ref[...] = (rstd_c * (gy_c - mean_c - xhat_c * prod_c))[:, 0:cn].astype(oc_ref.dtype)

    for q in dp_peers:
        for s in range(n_rep):
            at = q * n_rep + s
            arrived(cc.at[at], cc_recv.at[at], (e, q, s))
        other = q * n_rep + partner
        arrived(fa.at[other], fa_recv.at[other], (e, d, partner))
    beside = d * n_rep + partner
    arrived(cc.at[beside], cc_recv.at[beside], (e, d, partner))
    arrived(fa.at[beside], fa_recv.at[beside], (e, d, partner))

    for copy in sent:
        copy.wait_send()


def weight_kernel(
    scale, fa, cc, os_v, oc_v, gws_hbm, gwc_hbm, os_hbm, oc_hbm, gws_v, gwc_v, out_sem
):
    tokens = cc.shape[0] * cc.shape[1]
    cs, cn = gws_v.shape[0], gwc_v.shape[1]
    lo = round_up(cs)
    stores = [
        pltpu.make_async_copy(os_v, os_hbm, out_sem.at[0]),
        pltpu.make_async_copy(oc_v, oc_hbm, out_sem.at[1]),
        pltpu.make_async_copy(gws_v, gws_hbm, out_sem.at[2]),
        pltpu.make_async_copy(gwc_v, gwc_hbm, out_sem.at[3]),
    ]
    stores[0].start()
    stores[1].start()
    cot_all = cc[...].reshape(tokens, cc.shape[2])
    over_rows = (((0,), (0,)), ((), ()))
    gws_v[...] = (
        lax.dot_general(
            fa[:, :, 0:lo].reshape(tokens, lo),
            cot_all,
            over_rows,
            preferred_element_type=jnp.float32,
        )[0:cs, :]
        * scale
    )
    stores[2].start()
    gwc_v[...] = (
        lax.dot_general(
            cot_all,
            fa[:, :, lo:].reshape(tokens, fa.shape[2] - lo),
            over_rows,
            preferred_element_type=jnp.float32,
        )[:, 0:cn]
        * scale
    )
    stores[3].start()
    for store in stores:
        store.wait()


def gather_shards(
    feat_sig,
    feat_cnx,
    cotangent,
    w_sig,
    w_cnx,
    lengths,
    enc_of,
    owner_of,
    pre_sig,
    pre_cnx,
    gain_sig,
    gain_cnx,
):
    n_enc, n_dp, n_rep = (lax.axis_size(axis) for axis in ("enc", "dp", "rep"))
    slots = lengths.shape[1]
    rows, chunk = cotangent.shape
    depth = rows // slots
    cs, cn = feat_sig.shape[1], feat_cnx.shape[1]
    whole = w_sig.shape[0]
    owners = n_dp * n_rep
    block = whole // owners
    joint = round_up(cs) + round_up(cn)
    bf16, f32 = jnp.bfloat16, jnp.float32
    dma = pltpu.SemaphoreType.DMA
    scratch = [
        pltpu.SMEM((1, slots), jnp.int32),
        pltpu.SMEM((1, slots), jnp.int32),
        pltpu.SMEM((1, slots), jnp.int32),
        pltpu.VMEM((rows, chunk), bf16),
        pltpu.VMEM((rows, cs), bf16),
        pltpu.VMEM((rows, cn), bf16),
        pltpu.VMEM((rows, cs), bf16),
        pltpu.VMEM((rows, cn), bf16),
        pltpu.VMEM((cs,), f32),
        pltpu.VMEM((cn,), f32),
        pltpu.VMEM((cs, whole), bf16),
        pltpu.VMEM((whole, cn), bf16),
        pltpu.VMEM((n_enc, rows, chunk), bf16),
        pltpu.VMEM((n_dp, depth, joint), bf16),
        pltpu.VMEM((n_dp, depth, joint), bf16),
        pltpu.VMEM((n_enc, rows, LANES), f32),
        pltpu.VMEM((n_enc, rows, LANES), f32),
        pltpu.VMEM((rows, joint), f32),
        pltpu.VMEM((rows, joint), f32),
        pltpu.VMEM((rows, joint), f32),
        dma((10,)),
        dma((2 * n_enc,)),
        dma((n_enc,)),
        dma((n_enc,)),
        dma((n_dp,)),
        dma((owners,)),
        dma((n_dp,)),
        dma((owners,)),
        dma((owners,)),
        dma((n_dp,)),
        dma((n_dp,)),
        dma((n_enc,)),
        dma((n_enc,)),
        dma((n_enc,)),
        dma((n_enc,)),
    ]
    hbm = pl.BlockSpec(memory_space=pltpu.HBM)
    vmem = pl.BlockSpec(memory_space=pltpu.VMEM)
    parts = pl.pallas_call(
        functools.partial(fused_kernel, (n_enc, n_dp, n_rep, slots, depth)),
        out_shape=(
            pltpu.VMEM((owners, rows, joint), bf16),
            pltpu.VMEM((owners, rows, block), bf16),
            pltpu.VMEM((rows, cs), bf16),
            pltpu.VMEM((rows, cn), bf16),
        ),
        in_specs=[hbm] * 12,
        out_specs=(vmem,) * 4,
        scratch_shapes=scratch,
        compiler_params=pltpu.CompilerParams(
            collective_id=0, has_side_effects=True, vmem_limit_bytes=VMEM_BYTES
        ),
        cost_estimate=pl.CostEstimate(
            flops=2 * rows * whole * (cs + cn),
            bytes_accessed=2 * whole * (cs + cn),
            transcendentals=2 * rows,
        ),
    )(
        lengths,
        enc_of,
        owner_of,
        cotangent,
        feat_sig,
        feat_cnx,
        pre_sig,
        pre_cnx,
        gain_sig,
        gain_cnx,
        w_sig.T,
        w_cnx,
    )
    grad_w_sig, *rest = pl.pallas_call(
        functools.partial(weight_kernel, 1.0 / math.sqrt(owners * rows)),
        out_shape=(
            jax.ShapeDtypeStruct((cs, block), f32),
            jax.ShapeDtypeStruct((block, cn), f32),
            jax.ShapeDtypeStruct((rows, cs), bf16),
            jax.ShapeDtypeStruct((rows, cn), bf16),
        ),
        in_specs=[vmem] * 4,
        out_specs=(hbm,) * 4,
        scratch_shapes=[pltpu.VMEM((cs, block), f32), pltpu.VMEM((block, cn), f32), dma((4,))],
        compiler_params=pltpu.CompilerParams(vmem_limit_bytes=VMEM_BYTES // 4),
        cost_estimate=pl.CostEstimate(
            flops=2 * rows * owners * block * (cs + cn),
            bytes_accessed=4 * block * (cs + cn),
            transcendentals=0,
        ),
    )(*parts)
    return (grad_w_sig.T, *rest)


def shards(feat_sig, feat_cnx, cotangent, w_sig, *others):
    n_enc, n_dp, n_rep = (lax.axis_size(axis) for axis in ("enc", "dp", "rep"))
    rows, chunk = cotangent.shape
    owners = n_dp * n_rep
    whole = w_sig.shape[0]
    gathered = owners * rows * (feat_sig.shape[1] + feat_cnx.shape[1]) * 2
    fits = gathered <= GATHER_BYTES and n_rep == 2 and rows % 16 == 0
    fits = fits and others[1].shape[1] == n_dp and whole % (owners * LANES) == 0
    fits = fits and chunk % (whole // owners) == 0
    form = gather_shards if fits else partial_sum_shards
    return form(feat_sig, feat_cnx, cotangent, w_sig, *others)


def solution(mesh):
    in_specs = (
        P(("dp", "rep"), "enc"),
        P(("dp", "rep"), "enc"),
        P(("dp", "rep"), "enc"),
        P(None, "enc"),
        P(None, "enc"),
        P(("dp", "rep"), None),
        P(("dp", "rep"), None),
        P(("dp", "rep"), None),
        P(("dp", "rep"), "enc"),
        P(("dp", "rep"), "enc"),
        P("enc"),
        P("enc"),
    )
    out_specs = (
        P(("dp", "rep"), "enc"),
        P(("dp", "rep"), "enc"),
        P(("dp", "rep"), "enc"),
        P(("dp", "rep"), "enc"),
    )
    return jax.shard_map(shards, mesh=mesh, in_specs=in_specs, out_specs=out_specs, check_vma=False)
```
